512 devices in a mesh: dp: 64 (over y, z), tower: 2 (over x_hi), tensor: 4 (over x_lo, core).
Axes of the slice: x: 4 (x_hi: 2, x_lo: 2; x = x_hi * 2 + x_lo), y: 8, z: 8, core: 2. Of those that a mesh axis runs over, the one named last changes fastest.
Arguments:
- image_feats: bfloat16 [16384, 3200], P('dp', ('tower', 'tensor')), may hold values from -200 to 200
- text_feats: bfloat16 [16384, 4096], P('dp', ('tower', 'tensor')), may hold values from -200 to 200
- image_proj: bfloat16 [3200, 768], P(('tower', 'tensor')), may hold values from -0.109375 to 0.109375
- text_proj: bfloat16 [4096, 768], P(('tower', 'tensor')), may hold values from -0.09375 to 0.09375
- labels: int32 [16384], P('dp'), may hold values from 0 to 16383, as said below
- logit_scale: float32 [1], replicated, may hold values from 2 to 8
- logit_bias: float32 [1], replicated, may hold values from -4 to -1
Outputs:
- image_grad: bfloat16 [16384, 3200], P('dp', ('tower', 'tensor'))
- text_grad: bfloat16 [16384, 4096], P('dp', ('tower', 'tensor'))
- image_proj_grad: float32 [3200, 768], P(('tower', 'tensor'), 'dp')
- text_proj_grad: float32 [4096, 768], P(('tower', 'tensor'), 'dp')
The draws below stay inside these ranges and needn't reach their ends.
Inputs may be any that keep to these rules, and one draw needn't show every extreme that they name: `labels`: an image row of block j (rows j * 256 to (j + 1) * 256 - 1) has its positive text row in block (j - k) mod 64 for some 0 <= k < 4.
All inputs are finite; a program needn't handle non-finite values.
Results may differ from the reference program's by a relative error of at most 0.03.
Values may be sent and summed in bfloat16 or wider, within the bound.
No kernel may reach another device: no remote copies, remote signals or barrier semaphores. Data moves between devices by JAX's collectives and lax.ppermute only.
A program may use at most 64 MiB of HBM per device.

```python
import math
import jax
import jax.numpy as jnp
from jax import lax

D_IMG = 3200
D_TXT = 4096
EMBED = 768
TOK_DEV = 256
STEPS = 4
TOKENS = 16384
N_DP = 64
N_TOWER = 2
N_TENSOR = 4


def scaled_rows(base, key, row_count, col_count):
    row_key, col_key = jax.random.split(key)
    row_scale = jnp.exp(jax.random.uniform(row_key, (row_count, 1), jnp.float32) * math.log(10.0))
    ramp = jnp.arange(col_count, dtype=jnp.float32) / max(col_count - 1, 1)
    col_scale = jnp.exp(ramp * math.log(3.0))[None, :] * jnp.exp(jax.random.uniform(col_key, (1, col_count), jnp.float32, -0.4, 0.4))
    return base * row_scale * col_scale


def draw_image_feats(key, part):
    key = jax.random.fold_in(key, 11)
    base_key, scale_key = jax.random.split(key)
    base = jnp.clip(jax.random.normal(base_key, (TOKENS, D_IMG), jnp.float32), -4.0, 4.0)
    return scaled_rows(base, scale_key, TOKENS, D_IMG).astype(jnp.bfloat16)


def draw_text_feats(key, part):
    key = jax.random.fold_in(key, 12)
    base_key, scale_key = jax.random.split(key)
    base = jnp.clip(jax.random.normal(base_key, (TOKENS, D_TXT), jnp.float32), -4.0, 4.0)
    return scaled_rows(base, scale_key, TOKENS, D_TXT).astype(jnp.bfloat16)


def draw_labels(key, part):
    key = jax.random.fold_in(key, 13)
    offset_key, row_key = jax.random.split(key)
    offsets = jax.random.randint(offset_key, (TOKENS,), 0, STEPS)
    within = jax.random.randint(row_key, (TOKENS,), 0, TOK_DEV)
    block_ids = jnp.arange(TOKENS, dtype=jnp.int32) // TOK_DEV
    return (jnp.mod(block_ids - offsets, N_DP) * TOK_DEV + within).astype(jnp.int32)


def block_levels(stream_key, shape, cuts, low, high):
    gain, own = 1.0, jax.random.fold_in(stream_key, 6)
    for dim, parts in cuts:
        steps = jnp.exp(jax.random.uniform(jax.random.fold_in(own, dim), (parts,), jnp.float32, low / len(cuts), high / len(cuts)))
        gain = gain * jnp.repeat(steps, shape[dim] // parts).reshape([-1 if axis == dim else 1 for axis in range(len(shape))])
    return gain


def normal_values(stream_key, dims, deviation, most, cuts=(), kind=jnp.bfloat16):
    factor_of = block_levels(stream_key, dims, cuts, -0.22, 0.18) if cuts else 1.0
    array = jax.random.normal(stream_key, dims, jnp.float32) * deviation * factor_of
    return jnp.minimum(jnp.maximum(array, -most), most).astype(kind)


def setup_inputs(seed: int = 0) -> dict:
    arg_keys = jax.random.split(jax.random.key(seed), 8)
    image_feats = draw_image_feats(jax.random.fold_in(arg_keys[7], 71), 0)
    text_feats = draw_text_feats(jax.random.fold_in(arg_keys[7], 71), 0)
    image_proj = normal_values(arg_keys[2], (D_IMG, EMBED), D_IMG ** -0.5, 0.109375, ((0, 8),))
    text_proj = normal_values(arg_keys[3], (D_TXT, EMBED), D_TXT ** -0.5, 0.09375, ((0, 8),))
    labels = draw_labels(jax.random.fold_in(arg_keys[7], 71), 0)
    logit_scale = jnp.clip(jnp.exp(jax.random.uniform(arg_keys[5], (1,), jnp.float32, math.log(2.0), math.log(8.0))), 2.0, 8.0)
    logit_bias = jnp.clip(jax.random.uniform(arg_keys[6], (1,), jnp.float32, -4.0, -1.0), -4.0, -1.0)
    return {"image_feats": image_feats, "text_feats": text_feats, "image_proj": image_proj, "text_proj": text_proj, "labels": labels, "logit_scale": logit_scale, "logit_bias": logit_bias}


norm_eps = 1e-06

def project(feats, weights, groups):
    col_count = feats.shape[1] // groups
    summed = jnp.zeros((feats.shape[0], weights.shape[1]), jnp.float32)
    for member in range(groups):
        term_part = jnp.dot(feats[:, member * col_count:(member + 1) * col_count], weights[member * col_count:(member + 1) * col_count], preferred_element_type=jnp.float32)
        summed = summed + lax.optimization_barrier(term_part.astype(jnp.bfloat16)).astype(jnp.float32)
    return summed

def unit_rows(summed):
    length = jnp.sqrt(lax.optimization_barrier(jnp.sum(summed * summed, axis=1, keepdims=True)) + norm_eps)
    return (summed / length, length)

def backward(feats, weights, unit, length, grad_embed):
    grad_summed = ((grad_embed - unit * lax.optimization_barrier(jnp.sum(unit * grad_embed, axis=1, keepdims=True))) / length).astype(jnp.bfloat16)
    weight_grad = jnp.dot(feats.T, grad_summed, preferred_element_type=jnp.float32)
    feats_grad = jnp.dot(grad_summed, weights.T, preferred_element_type=jnp.float32).astype(jnp.bfloat16)
    return (feats_grad, weight_grad)

def contrast(embed_img, embed_txt, labels, scale_value, bias_value):
    row_count = TOK_DEV

    def block_step(text_acc, block_index):
        first_row = (block_index * row_count).astype(jnp.int32)
        image_rows = lax.dynamic_slice_in_dim(embed_img, first_row, row_count, 0)
        row_labels = lax.dynamic_slice_in_dim(labels, first_row, row_count, 0)
        row_grad = jnp.zeros((row_count, embed_img.shape[1]), jnp.float32)
        for offset in range(STEPS):
            source = jnp.mod(block_index - offset, N_DP).astype(jnp.int32)
            text_first = (source * row_count).astype(jnp.int32)
            text_rows = lax.dynamic_slice_in_dim(embed_txt, text_first, row_count, 0)
            col_ids = text_first + jnp.arange(row_count, dtype=jnp.int32)
            polarity = jnp.where(row_labels[:, None] == col_ids[None, :], 1.0, -1.0).astype(jnp.float32)
            logits = scale_value * jnp.dot(image_rows, text_rows.T, preferred_element_type=jnp.float32) + bias_value
            weights = (-scale_value * polarity * jax.nn.sigmoid(-polarity * logits) / row_count).astype(jnp.bfloat16)
            row_grad = row_grad + jnp.dot(weights, text_rows, preferred_element_type=jnp.float32)
            partial_value = jnp.dot(weights.T, image_rows, preferred_element_type=jnp.float32)
            current = lax.dynamic_slice_in_dim(text_acc, text_first, row_count, 0)
            text_acc = lax.dynamic_update_slice_in_dim(text_acc, current + partial_value, text_first, 0)
        return (text_acc, row_grad)
    text_acc, row_grads = lax.scan(block_step, jnp.zeros(embed_txt.shape, jnp.float32), jnp.arange(N_DP, dtype=jnp.int32))
    return (row_grads.reshape(embed_img.shape), text_acc)

def reference(image_feats, text_feats, image_proj, text_proj, labels, logit_scale, logit_bias):
    groups = N_TOWER * N_TENSOR
    img_unit, img_length = unit_rows(project(image_feats, image_proj, groups))
    txt_unit, txt_length = unit_rows(project(text_feats, text_proj, groups))
    grad_img, grad_txt = contrast(img_unit.astype(jnp.bfloat16), txt_unit.astype(jnp.bfloat16), labels, logit_scale[0], logit_bias[0])
    image_grad, image_proj_grad = backward(image_feats, image_proj, img_unit, img_length, grad_img)
    text_grad, text_proj_grad = backward(text_feats, text_proj, txt_unit, txt_length, grad_txt)
    return (image_grad, text_grad, image_proj_grad, text_proj_grad)
```

```python
import jax
import jax.numpy as jnp
from jax import lax
from jax.sharding import Mesh, PartitionSpec as P

STEPS = 4
NORM_EPS = 1e-06
X = ("xh", "xl", "core")
DP = ("y", "z")


def shifted(value, steps):
    count = lax.axis_size(DP)
    pairs = [(source, (source + steps) % count) for source in range(count)]
    return lax.ppermute(value, DP, pairs)


def on_device(image_feats, text_feats, image_proj, text_proj, labels, logit_scale, logit_bias):
    bf16, f32 = jnp.bfloat16, jnp.float32
    groups = lax.axis_size(X)
    member = lax.axis_index(X)
    anchor = lax.axis_index(DP)
    blocks = lax.axis_size(DP)
    ny, nz = lax.axis_size("y"), lax.axis_size("z")
    rows = image_feats.shape[0]
    share = rows // groups
    d_img, d_txt = image_feats.shape[1], text_feats.shape[1]
    embed = image_proj.shape[1]
    img_line = lax.all_gather(image_feats, "y", axis=0, tiled=True)
    txt_line = lax.all_gather(text_feats, "y", axis=0, tiled=True)
    img_part = jnp.dot(image_feats, image_proj, preferred_element_type=f32).astype(bf16)
    txt_part = jnp.dot(text_feats, text_proj, preferred_element_type=f32).astype(bf16)
    parts = jnp.concatenate(
        [img_part.reshape(groups, share, embed), txt_part.reshape(groups, share, embed)], axis=1
    )
    parts = lax.all_to_all(parts, X, 0, 0, tiled=True)
    summed = jnp.sum(parts.astype(f32), axis=0)
    length = jnp.sqrt(jnp.sum(summed * summed, axis=1, keepdims=True) + NORM_EPS)
    unit = summed / length
    emb = unit.astype(bf16)
    img_own, txt_own = emb[:share], emb[share:]
    near = shifted(txt_own, 1)
    img_all = lax.all_gather(img_own, X, axis=0, tiled=True)
    pair = jnp.concatenate([txt_own, near])
    far = shifted(pair, 2)
    cols = jnp.concatenate([pair, far])
    offsets = jnp.arange(STEPS, dtype=jnp.int32)
    col_ids = (
        jnp.mod(anchor - offsets, blocks)[:, None] * rows
        + member * share
        + jnp.arange(share, dtype=jnp.int32)[None, :]
    ).reshape(-1)
    scale_value, bias_value = logit_scale[0], logit_bias[0]
    polarity = jnp.where(labels[:, None] == col_ids[None, :], 1.0, -1.0).astype(f32)
    logits = (
        scale_value
        * lax.dot_general(img_all, cols, (((1,), (1,)), ((), ())), preferred_element_type=f32)
        + bias_value
    )
    weights = (-scale_value * polarity * jax.nn.sigmoid(-polarity * logits) / rows).astype(bf16)
    txt_terms = lax.dot_general(weights, img_all, (((0,), (0,)), ((), ())), preferred_element_type=f32)
    img_terms = jnp.dot(weights, cols, preferred_element_type=f32).astype(bf16)
    back = shifted(txt_terms[2 * share :].astype(bf16), -2)
    img_terms = lax.all_to_all(img_terms.reshape(groups, share, embed), X, 0, 0, tiled=True)
    two = txt_terms[: 2 * share] + back.astype(f32)
    last = shifted(two[share:].astype(bf16), -1)
    grad_txt = two[:share] + last.astype(f32)
    grad_img = jnp.sum(img_terms.astype(f32), axis=0)
    grad = jnp.concatenate([grad_img, grad_txt])
    grad_summed = ((grad - unit * jnp.sum(unit * grad, axis=1, keepdims=True)) / length).astype(bf16)
    wide = embed // ny
    by_cols = grad_summed.reshape(2 * share, ny, wide).transpose(1, 0, 2)
    by_cols = lax.all_to_all(by_cols, "y", 0, 0, tiled=True)
    by_cols = by_cols.transpose(1, 0, 2).reshape(2 * share, embed)
    both = lax.all_gather(jnp.concatenate([grad_summed, by_cols]), X, axis=0, tiled=False)
    img_rows = both[:, :share].reshape(rows, embed)
    txt_rows = both[:, share : 2 * share].reshape(rows, embed)

    def line(part):
        return part.reshape(groups * share, ny, wide).transpose(1, 0, 2).reshape(ny * rows, wide)

    img_cols = line(both[:, 2 * share : 3 * share])
    txt_cols = line(both[:, 3 * share :])
    down = (((0,), (0,)), ((), ()))
    img_wgrad = lax.dot_general(img_cols, img_line, down, preferred_element_type=f32)
    txt_wgrad = lax.dot_general(txt_cols, txt_line, down, preferred_element_type=f32)
    wgrad = jnp.concatenate([img_wgrad, txt_wgrad], axis=1).astype(bf16)
    wgrad = lax.all_to_all(wgrad.reshape(nz, wide // nz, d_img + d_txt), "z", 0, 0, tiled=True)
    wgrad = jnp.sum(wgrad.astype(f32), axis=0)
    across = (((1,), (1,)), ((), ()))
    image_grad = lax.dot_general(img_rows, image_proj, across, preferred_element_type=f32).astype(bf16)
    text_grad = lax.dot_general(txt_rows, text_proj, across, preferred_element_type=f32).astype(bf16)
    return (image_grad, text_grad, wgrad[:, :d_img].T, wgrad[:, d_img:].T)


def solution(mesh):
    fine = Mesh(mesh.devices.reshape(8, 8, 2, 2, 2), ("y", "z", "xh", "xl", "core"))
    placed = (P(DP, X), P(DP, X), P(X, None), P(X, None), P(DP), P(), P())
    return jax.shard_map(
        on_device,
        mesh=fine,
        in_specs=placed,
        out_specs=(P(DP, X), P(DP, X), P(X, DP), P(X, DP)),
        check_vma=False,
    )
```

```python
import jax
import jax.numpy as jnp
from jax import lax
from jax.experimental import pallas as pl
from jax.experimental.pallas import tpu as pltpu
from jax.sharding import Mesh, PartitionSpec as P

STEPS = 4
NORM_EPS = 1e-06
X = ("xh", "xl", "core")
DP = ("y", "z")
ACROSS = (((1,), (1,)), ((), ()))
DOWN = (((0,), (0,)), ((), ()))
HALF = 256


def shifted(value, steps):
    count = lax.axis_size(DP)
    pairs = [(source, (source + steps) % count) for source in range(count)]
    return lax.ppermute(value, DP, pairs)


def project_kernel(img_t_ref, txt_ref, img_proj_ref, txt_proj_ref, parts_ref, pack_ref):
    f32, bf16 = jnp.float32, jnp.bfloat16
    groups, share = parts_ref.shape[0], parts_ref.shape[1] // 2
    d_txt, d_img = txt_ref.shape[1], img_t_ref.shape[0]
    for half in range(d_txt // HALF):
        pack_ref[half * HALF : (half + 1) * HALF] = txt_ref[:, half * HALF : (half + 1) * HALF]
    pack_ref[d_txt:] = img_t_ref[...]
    txt = jnp.dot(txt_ref[...], txt_proj_ref[...], preferred_element_type=f32).astype(bf16)
    img = lax.dot_general(img_t_ref[...], img_proj_ref[...], DOWN, preferred_element_type=f32)
    img = img.astype(bf16)
    for member in range(groups):
        rows = slice(member * share, (member + 1) * share)
        parts_ref[member, :share] = img[rows]
        parts_ref[member, share:] = txt[rows]


def project(image_feats_t, text_feats, image_proj, text_proj, groups):
    rows, d_txt = text_feats.shape
    d_img, embed = image_proj.shape
    return pl.pallas_call(
        project_kernel,
        out_shape=(
            jax.ShapeDtypeStruct((groups, 2 * rows // groups, embed), jnp.bfloat16),
            jax.ShapeDtypeStruct((d_txt + d_img, HALF), jnp.bfloat16),
        ),
        compiler_params=pltpu.CompilerParams(vmem_limit_bytes=58 * 1024 * 1024),
        cost_estimate=pl.CostEstimate(
            flops=2 * rows * (d_img + d_txt) * embed, bytes_accessed=4_000_000, transcendentals=0
        ),
        name="project",
    )(image_feats_t, text_feats, image_proj, text_proj)


def wgrad_kernel(cols_ref, line_ref, out_ref, total_ref):
    f32 = jnp.float32
    step = pl.program_id(0)
    groups, _, both, wide = cols_ref.shape
    share = both // 2
    d_all = total_ref.shape[1]
    d_txt = 2 * HALF

    @pl.when(step == 0)
    def _():
        total_ref[...] = jnp.zeros_like(total_ref)

    for k in range(line_ref.shape[0]):
        img_cols = cols_ref[:, k, :share].reshape(groups * share, wide)
        txt_cols = cols_ref[:, k, share:].reshape(groups * share, wide)
        total_ref[:, d_txt:] += lax.dot_general(
            img_cols, line_ref[k, d_txt:], (((0,), (1,)), ((), ())), preferred_element_type=f32
        )
        for half in range(d_txt // HALF):
            lanes = slice(half * HALF, (half + 1) * HALF)
            total_ref[:, lanes] += lax.dot_general(
                txt_cols,
                line_ref[k, half * HALF : (half + 1) * HALF],
                DOWN,
                preferred_element_type=f32,
            )

    @pl.when(step == pl.num_programs(0) - 1)
    def _():
        parts, padded, _ = out_ref.shape
        take = wide // parts
        for part in range(parts):
            out_ref[part, :take] = total_ref[part * take : (part + 1) * take].astype(out_ref.dtype)
            out_ref[part, take:] = jnp.zeros((padded - take, d_all), out_ref.dtype)


def project_grads(cols, line, parts):
    groups, ny, both, wide = cols.shape
    d_all = line.shape[1]
    padded = 16
    per = 2
    return pl.pallas_call(
        wgrad_kernel,
        grid=(ny // per,),
        in_specs=[
            pl.BlockSpec((groups, per, both, wide), lambda i: (0, i, 0, 0)),
            pl.BlockSpec((per, d_all, HALF), lambda i: (i, 0, 0)),
        ],
        out_specs=pl.BlockSpec((parts, padded, d_all), lambda i: (0, 0, 0)),
        out_shape=jax.ShapeDtypeStruct((parts, padded, d_all), jnp.bfloat16),
        scratch_shapes=[pltpu.VMEM((wide, d_all), jnp.float32)],
        compiler_params=pltpu.CompilerParams(vmem_limit_bytes=58 * 1024 * 1024),
        cost_estimate=pl.CostEstimate(
            flops=4 * ny * HALF * wide * d_all, bytes_accessed=5_000_000, transcendentals=0
        ),
        name="project_grads",
    )(cols, line)


def on_device(image_feats, text_feats, image_proj, text_proj, labels, logit_scale, logit_bias):
    bf16, f32 = jnp.bfloat16, jnp.float32
    groups = lax.axis_size(X)
    member = lax.axis_index(X)
    anchor = lax.axis_index(DP)
    blocks = lax.axis_size(DP)
    ny, nz = lax.axis_size("y"), lax.axis_size("z")
    rows = image_feats.shape[0]
    share = rows // groups
    d_img, d_txt = image_feats.shape[1], text_feats.shape[1]
    embed = image_proj.shape[1]
    parts, pack = project(image_feats.T, text_feats, image_proj, text_proj, groups)
    line = lax.all_gather(pack, "y", axis=0, tiled=False)
    parts = lax.all_to_all(parts, X, 0, 0, tiled=True)
    summed = jnp.sum(parts.astype(f32), axis=0)
    length = jnp.sqrt(jnp.sum(summed * summed, axis=1, keepdims=True) + NORM_EPS)
    unit = summed / length
    emb = unit.astype(bf16)
    img_own, txt_own = emb[:share], emb[share:]
    img_all = jnp.broadcast_to(img_own[None], (groups, share, embed))
    img_all = lax.all_to_all(img_all, X, 0, 0, tiled=True).reshape(rows, embed)
    near = shifted(txt_own, 1)
    pair = jnp.concatenate([txt_own, near])
    far = shifted(pair, 2)
    cols = jnp.concatenate([pair, far])
    offsets = jnp.arange(STEPS, dtype=jnp.int32)
    col_ids = (
        jnp.mod(anchor - offsets, blocks)[:, None] * rows
        + member * share
        + jnp.arange(share, dtype=jnp.int32)[None, :]
    ).reshape(-1)
    scale_value, bias_value = logit_scale[0], logit_bias[0]
    polarity = jnp.where(labels[:, None] == col_ids[None, :], 1.0, -1.0).astype(f32)
    logits = (
        scale_value * lax.dot_general(img_all, cols, ACROSS, preferred_element_type=f32)
        + bias_value
    )
    weights = (-scale_value * polarity * jax.nn.sigmoid(-polarity * logits) / rows).astype(bf16)
    txt_terms = lax.dot_general(weights, img_all, DOWN, preferred_element_type=f32)
    img_terms = jnp.dot(weights, cols, preferred_element_type=f32).astype(bf16)
    back = shifted(txt_terms[2 * share :].astype(bf16), -2)
    img_terms = lax.all_to_all(img_terms.reshape(groups, share, embed), X, 0, 0, tiled=True)
    two = txt_terms[: 2 * share] + back.astype(f32)
    last = shifted(two[share:].astype(bf16), -1)
    grad_txt = two[:share] + last.astype(f32)
    grad_img = jnp.sum(img_terms.astype(f32), axis=0)
    grad = jnp.concatenate([grad_img, grad_txt])
    grad_summed = ((grad - unit * jnp.sum(unit * grad, axis=1, keepdims=True)) / length).astype(bf16)
    wide = embed // ny
    by_cols = grad_summed.reshape(2 * share, ny, wide).transpose(1, 0, 2)
    by_cols = lax.all_to_all(by_cols, "y", 0, 0, tiled=True)
    padded = jnp.pad(grad_summed, ((0, share), (0, 0)))
    by_cols, padded, line = lax.optimization_barrier((by_cols, padded, line))
    cols_all = lax.all_gather(by_cols, X, axis=0, tiled=False)
    wgrad = project_grads(cols_all, line, nz)
    wgrad = lax.all_to_all(wgrad, "z", 0, 0, tiled=True)
    wgrad = jnp.sum(wgrad[:, : wide // nz].astype(f32), axis=0)
    rows_all = lax.all_gather(padded, X, axis=0, tiled=False)
    img_rows = rows_all[:, :share].reshape(rows, embed)
    txt_rows = rows_all[:, share : 2 * share].reshape(rows, embed)
    image_grad = lax.dot_general(img_rows, image_proj, ACROSS, preferred_element_type=f32).astype(bf16)
    text_grad = lax.dot_general(txt_rows, text_proj, ACROSS, preferred_element_type=f32).astype(bf16)
    return (image_grad, text_grad, wgrad[:, d_txt:].T, wgrad[:, :d_txt].T)


def solution(mesh):
    fine = Mesh(mesh.devices.reshape(8, 8, 2, 2, 2), ("y", "z", "xh", "xl", "core"))
    placed = (P(DP, X), P(DP, X), P(X, None), P(X, None), P(DP), P(), P())
    return jax.shard_map(
        on_device,
        mesh=fine,
        in_specs=placed,
        out_specs=(P(DP, X), P(DP, X), P(X, DP), P(X, DP)),
        check_vma=False,
    )
```

```python
import jax
import jax.numpy as jnp
from jax import lax
from jax.experimental import pallas as pl
from jax.experimental.pallas import tpu as pltpu
from jax.sharding import Mesh, PartitionSpec as P

STEPS = 4
NORM_EPS = 1e-06
X = ("xh", "xl", "core")
DP = ("y", "z")
ACROSS = (((1,), (1,)), ((), ()))
DOWN = (((0,), (0,)), ((), ()))
HALF = 256
VMEM = 58 * 1024 * 1024


def shifted(value, steps):
    count = lax.axis_size(DP)
    pairs = [(source, (source + steps) % count) for source in range(count)]
    return lax.ppermute(value, DP, pairs)


def along(value, axis, steps):
    count = lax.axis_size(axis)
    return lax.ppermute(value, axis, [(source, (source + steps) % count) for source in range(count)])


def project_kernel(img_t_ref, txt_ref, img_proj_ref, txt_proj_ref, parts_ref, pack_ref):
    f32, bf16 = jnp.float32, jnp.bfloat16
    groups, share = parts_ref.shape[0], parts_ref.shape[1] // 2
    d_txt, d_img = txt_ref.shape[1], img_t_ref.shape[0]
    for half in range(d_txt // HALF):
        pack_ref[half * HALF : (half + 1) * HALF] = txt_ref[:, half * HALF : (half + 1) * HALF]
    pack_ref[d_txt:] = img_t_ref[...]
    txt = jnp.dot(txt_ref[...], txt_proj_ref[...], preferred_element_type=f32).astype(bf16)
    img = lax.dot_general(img_t_ref[...], img_proj_ref[...], DOWN, preferred_element_type=f32)
    img = img.astype(bf16)
    for member in range(groups):
        rows = slice(member * share, (member + 1) * share)
        parts_ref[member, :share] = img[rows]
        parts_ref[member, share:] = txt[rows]


def project(image_feats_t, text_feats, image_proj, text_proj, groups):
    rows, d_txt = text_feats.shape
    d_img, embed = image_proj.shape
    return pl.pallas_call(
        project_kernel,
        out_shape=(
            jax.ShapeDtypeStruct((groups, 2 * rows // groups, embed), jnp.bfloat16),
            jax.ShapeDtypeStruct((d_txt + d_img, HALF), jnp.bfloat16),
        ),
        compiler_params=pltpu.CompilerParams(vmem_limit_bytes=VMEM),
        cost_estimate=pl.CostEstimate(
            flops=2 * rows * (d_img + d_txt) * embed, bytes_accessed=4_000_000, transcendentals=0
        ),
        name="project",
    )(image_feats_t, text_feats, image_proj, text_proj)


def wgrad_kernel(y_ref, cols_ref, *refs):
    f32 = jnp.float32
    lines, (out_ref,) = refs[:-1], refs[-1:]
    groups, ny, both, wide = cols_ref.shape
    share = both // 2
    d_all = out_ref.shape[2]
    d_txt = 2 * HALF
    totals = [None] * 3
    for line_ref, back in zip(lines, (0, 1, -1, 2, -2, 3, -3, 4)):
        source = lax.rem(y_ref[0] + (ny - back), ny)
        img_cols = cols_ref[:, source, :share].reshape(groups * share, wide)
        txt_cols = cols_ref[:, source, share:].reshape(groups * share, wide)
        terms = [
            lax.dot_general(
                txt_cols, line_ref[:HALF], DOWN, preferred_element_type=f32
            ),
            lax.dot_general(
                txt_cols, line_ref[HALF:d_txt], DOWN, preferred_element_type=f32
            ),
            lax.dot_general(
                img_cols, line_ref[d_txt:], (((0,), (1,)), ((), ())), preferred_element_type=f32
            ),
        ]
        totals = [term if total is None else total + term for total, term in zip(totals, terms)]
    parts, padded, _ = out_ref.shape
    take = wide // parts
    starts = (0, HALF, d_txt, d_all)
    for part in range(parts):
        for piece in range(3):
            lanes = slice(starts[piece], starts[piece + 1])
            out_ref[part, :take, lanes] = totals[piece][part * take : (part + 1) * take].astype(
                out_ref.dtype
            )
        out_ref[part, take:] = jnp.zeros((padded - take, d_all), out_ref.dtype)


def project_grads(y_index, cols, lines, parts):
    groups, ny, both, wide = cols.shape
    d_all = lines[0].shape[0]
    padded = 16
    return pl.pallas_call(
        wgrad_kernel,
        in_specs=[pl.BlockSpec(memory_space=pltpu.SMEM)]
        + [pl.BlockSpec(memory_space=pltpu.VMEM)] * (1 + ny),
        out_shape=jax.ShapeDtypeStruct((parts, padded, d_all), jnp.bfloat16),
        compiler_params=pltpu.CompilerParams(vmem_limit_bytes=VMEM),
        cost_estimate=pl.CostEstimate(
            flops=4 * ny * HALF * wide * d_all, bytes_accessed=5_000_000, transcendentals=0
        ),
        name="project_grads",
    )(y_index, cols, *lines)


def feature_grads_kernel(
    member_ref, own_ref, core_ref, low_ref, high_ref, img_proj_ref, txt_proj_ref,
    img_ref, txt_ref, img_rows, txt_rows,
):
    share = own_ref.shape[0] // 2
    place = 0
    for ref in (own_ref, core_ref, low_ref, high_ref):
        for piece in range(ref.shape[0] // (2 * share)):
            row = pl.multiple_of((member_ref[0] ^ place) * share, share)
            first = piece * 2 * share
            img_rows[pl.ds(row, share)] = ref[first : first + share]
            txt_rows[pl.ds(row, share)] = ref[first + share : first + 2 * share]
            place += 1
    txt_ref[...] = lax.dot_general(
        txt_rows[...], txt_proj_ref[...], ACROSS, preferred_element_type=jnp.float32
    ).astype(txt_ref.dtype)
    img_ref[...] = lax.dot_general(
        img_proj_ref[...], img_rows[...], ACROSS, preferred_element_type=jnp.float32
    ).astype(img_ref.dtype)


def feature_grads(member, pieces, image_proj, text_proj, rows):
    d_img, embed = image_proj.shape
    d_txt = text_proj.shape[0]
    return pl.pallas_call(
        feature_grads_kernel,
        in_specs=[pl.BlockSpec(memory_space=pltpu.SMEM)]
        + [pl.BlockSpec(memory_space=pltpu.VMEM)] * 6,
        out_shape=(
            jax.ShapeDtypeStruct((d_img, rows), jnp.bfloat16),
            jax.ShapeDtypeStruct((rows, d_txt), jnp.bfloat16),
        ),
        scratch_shapes=[pltpu.VMEM((rows, embed), jnp.bfloat16)] * 2,
        compiler_params=pltpu.CompilerParams(vmem_limit_bytes=VMEM),
        cost_estimate=pl.CostEstimate(
            flops=2 * rows * (d_img + d_txt) * embed, bytes_accessed=4_000_000, transcendentals=0
        ),
        name="feature_grads",
    )(member, *pieces, image_proj, text_proj)


def on_device(image_feats, text_feats, image_proj, text_proj, labels, logit_scale, logit_bias):
    bf16, f32 = jnp.bfloat16, jnp.float32
    groups = lax.axis_size(X)
    member = lax.axis_index(X)
    anchor = lax.axis_index(DP)
    blocks = lax.axis_size(DP)
    ny, nz = lax.axis_size("y"), lax.axis_size("z")
    rows = image_feats.shape[0]
    share = rows // groups
    d_img, d_txt = image_feats.shape[1], text_feats.shape[1]
    embed = image_proj.shape[1]
    parts, pack = project(image_feats.T, text_feats, image_proj, text_proj, groups)
    up, down = along(pack, "y", 1), along(pack, "y", -1)
    parts = lax.all_to_all(parts, X, 0, 0, tiled=True)
    parts, up, down = lax.optimization_barrier((parts, up, down))
    summed = jnp.sum(parts.astype(f32), axis=0)
    length = jnp.sqrt(jnp.sum(summed * summed, axis=1, keepdims=True) + NORM_EPS)
    unit = summed / length
    emb = unit.astype(bf16)
    img_own, txt_own = emb[:share], emb[share:]
    img_all = jnp.broadcast_to(img_own[None], (groups, share, embed))
    img_all = lax.all_to_all(img_all, X, 0, 0, tiled=True).reshape(rows, embed)
    near = shifted(txt_own, 1)
    pair = jnp.concatenate([txt_own, near])
    pair, up, down = lax.optimization_barrier((pair, up, down))
    far = shifted(pair, 2)
    up2, down2 = along(up, "y", 1), along(down, "y", -1)
    cols = jnp.concatenate([pair, far])
    offsets = jnp.arange(STEPS, dtype=jnp.int32)
    col_ids = (
        jnp.mod(anchor - offsets, blocks)[:, None] * rows
        + member * share
        + jnp.arange(share, dtype=jnp.int32)[None, :]
    ).reshape(-1)
    scale_value, bias_value = logit_scale[0], logit_bias[0]
    polarity = jnp.where(labels[:, None] == col_ids[None, :], 1.0, -1.0).astype(f32)
    logits = (
        scale_value * lax.dot_general(img_all, cols, ACROSS, preferred_element_type=f32)
        + bias_value
    )
    weights = (-scale_value * polarity * jax.nn.sigmoid(-polarity * logits) / rows).astype(bf16)
    txt_terms = lax.dot_general(weights, img_all, DOWN, preferred_element_type=f32)
    img_terms = jnp.dot(weights, cols, preferred_element_type=f32).astype(bf16)
    img_terms, up2, down2 = lax.optimization_barrier((img_terms, up2, down2))
    up3, down3 = along(up2, "y", 1), along(down2, "y", -1)
    back = shifted(txt_terms[2 * share :].astype(bf16), -2)
    img_terms = lax.all_to_all(img_terms.reshape(groups, share, embed), X, 0, 0, tiled=True)
    img_terms, up3, down3 = lax.optimization_barrier((img_terms, up3, down3))
    up4 = along(up3, "y", 1)
    two = txt_terms[: 2 * share] + back.astype(f32)
    last = shifted(two[share:].astype(bf16), -1)
    grad_txt = two[:share] + last.astype(f32)
    grad_img = jnp.sum(img_terms.astype(f32), axis=0)
    grad = jnp.concatenate([grad_img, grad_txt])
    grad_summed = ((grad - unit * jnp.sum(unit * grad, axis=1, keepdims=True)) / length).astype(bf16)
    wide = embed // ny
    by_cols = grad_summed.reshape(2 * share, ny, wide).transpose(1, 0, 2)
    by_cols = lax.all_to_all(by_cols, "y", 0, 0, tiled=True)
    pieces = [grad_summed]
    for axis in ("core", "xl", "xh"):
        pieces.append(along(jnp.concatenate(pieces) if len(pieces) > 1 else pieces[0], axis, 1))
    by_cols, up4 = lax.optimization_barrier((by_cols, up4))
    cols_all = jnp.broadcast_to(by_cols[None], (groups,) + by_cols.shape)
    cols_all = lax.all_to_all(cols_all, X, 0, 0, tiled=True)
    y_index = lax.axis_index("y").astype(jnp.int32).reshape(1)
    wgrad = project_grads(y_index, cols_all, (pack, up, down, up2, down2, up3, down3, up4), nz)
    wgrad = lax.all_to_all(wgrad, "z", 0, 0, tiled=True)
    wgrad = jnp.sum(wgrad[:, : wide // nz].astype(f32), axis=0)
    member_index = member.astype(jnp.int32).reshape(1)
    image_grad, text_grad = feature_grads(member_index, pieces, image_proj, text_proj, rows)
    return (image_grad.T, text_grad, wgrad[:, d_txt:].T, wgrad[:, :d_txt].T)


def solution(mesh):
    fine = Mesh(mesh.devices.reshape(8, 8, 2, 2, 2), ("y", "z", "xh", "xl", "core"))
    placed = (P(DP, X), P(DP, X), P(X, None), P(X, None), P(DP), P(), P())
    return jax.shard_map(
        on_device,
        mesh=fine,
        in_specs=placed,
        out_specs=(P(DP, X), P(DP, X), P(X, DP), P(X, DP)),
        check_vma=False,
    )
```

```python
import jax
import jax.numpy as jnp
from jax import lax
from jax.experimental import pallas as pl
from jax.experimental.pallas import tpu as pltpu
from jax.sharding import Mesh, PartitionSpec as P

STEPS = 4
NORM_EPS = 1e-06
X = ("xh", "xl", "core")
DP = ("yh", "yl", "z")
ACROSS = (((1,), (1,)), ((), ()))
DOWN = (((0,), (0,)), ((), ()))
HALF = 256
VMEM = 58 * 1024 * 1024
F32, BF16 = jnp.float32, jnp.bfloat16


def shifted(value, steps):
    count = lax.axis_size(DP)
    pairs = [(source, (source + steps) % count) for source in range(count)]
    return lax.ppermute(value, DP, pairs)


def swapped(value, axis, bits):
    count = lax.axis_size(axis)
    return lax.ppermute(value, axis, [(source, source ^ bits) for source in range(count)])


def call(kernel, name, out_shape, args, flops, scratch=(), scalars=0):
    spaces = [pltpu.SMEM] * scalars + [pltpu.VMEM] * (len(args) - scalars)
    return pl.pallas_call(
        kernel,
        out_shape=out_shape,
        in_specs=[pl.BlockSpec(memory_space=space) for space in spaces],
        scratch_shapes=list(scratch),
        compiler_params=pltpu.CompilerParams(vmem_limit_bytes=VMEM),
        cost_estimate=pl.CostEstimate(flops=flops, bytes_accessed=4_000_000, transcendentals=0),
        name=name,
    )(*args)


def project_kernel(img_t_ref, txt_ref, img_proj_ref, txt_proj_ref, parts_ref, pack_ref):
    groups, share = parts_ref.shape[0], parts_ref.shape[1] // 2
    d_txt = txt_ref.shape[1]
    for half in range(d_txt // HALF):
        pack_ref[half * HALF : (half + 1) * HALF] = txt_ref[:, half * HALF : (half + 1) * HALF]
    pack_ref[d_txt:] = img_t_ref[...]
    txt = jnp.dot(txt_ref[...], txt_proj_ref[...], preferred_element_type=F32).astype(BF16)
    img = lax.dot_general(img_t_ref[...], img_proj_ref[...], DOWN, preferred_element_type=F32)
    img = img.astype(BF16)
    for member in range(groups):
        rows = slice(member * share, (member + 1) * share)
        parts_ref[member, :share] = img[rows]
        parts_ref[member, share:] = txt[rows]


def wgrad_kernel(place_ref, cols_ref, *refs):
    lines, out_ref, total_ref = refs[:-2], refs[-2], refs[-1]
    groups, quad, share, wide = cols_ref.shape
    wide //= 2
    d_all = lines[0].shape[0]
    d_txt = 2 * HALF
    d_img = d_all - d_txt
    sums = [None] * 3
    for bits, line_ref in enumerate(lines):
        cols = cols_ref[:, place_ref[0] ^ bits].reshape(groups * share, 2 * wide)
        cols = cols.T
        img_cols, txt_cols = cols[:wide], cols[wide:]
        terms = [
            jnp.dot(txt_cols, line_ref[:HALF], preferred_element_type=F32),
            jnp.dot(txt_cols, line_ref[HALF:d_txt], preferred_element_type=F32),
            lax.dot_general(img_cols, line_ref[d_txt:], ACROSS, preferred_element_type=F32),
        ]
        sums = [term if total is None else total + term for total, term in zip(sums, terms)]
    peers, height, _ = out_ref.shape
    take = height // 4
    for peer in range(peers):
        rows = slice(peer * take, (peer + 1) * take)
        total_ref[peer, :take] = sums[0][rows]
        total_ref[peer, take : 2 * take] = sums[1][rows]
        total_ref[peer, 2 * take : 3 * take] = sums[2][rows, :HALF]
        total_ref[peer, 3 * take :, : d_img - HALF] = sums[2][rows, HALF:]
        total_ref[peer, 3 * take :, d_img - HALF :] = jnp.zeros((take, 2 * HALF - d_img), F32)
    out_ref[...] = total_ref[...].astype(BF16)


def total_kernel(blocks_ref, img_ref, txt_ref, total_ref):
    take = img_ref.shape[0]
    d_img = img_ref.shape[1]
    total = blocks_ref[0].astype(F32)
    for peer in range(1, blocks_ref.shape[0]):
        total = total + blocks_ref[peer].astype(F32)
    total_ref[...] = total
    txt_ref[:, :HALF] = total_ref[:take]
    txt_ref[:, HALF:] = total_ref[take : 2 * take]
    img_ref[:, :HALF] = total_ref[2 * take : 3 * take]
    img_ref[:, HALF:] = total_ref[3 * take :, : d_img - HALF]


def feature_grads_kernel(rows_ref, img_proj_ref, txt_proj_ref, img_ref, txt_ref):
    groups, share, embed = rows_ref.shape
    share //= 2
    img_rows = rows_ref[:, :share].reshape(groups * share, embed)
    txt_rows = rows_ref[:, share:].reshape(groups * share, embed)
    txt_ref[...] = lax.dot_general(
        txt_rows, txt_proj_ref[...], ACROSS, preferred_element_type=F32
    ).astype(BF16)
    img_ref[...] = lax.dot_general(
        img_proj_ref[...], img_rows, ACROSS, preferred_element_type=F32
    ).astype(BF16)


def on_device(image_feats, text_feats, image_proj, text_proj, labels, logit_scale, logit_bias):
    groups = lax.axis_size(X)
    member = lax.axis_index(X)
    anchor = lax.axis_index(DP)
    blocks = lax.axis_size(DP)
    quad = lax.axis_size("yl")
    peers = blocks // quad
    rows = image_feats.shape[0]
    share = rows // groups
    d_img, d_txt = image_feats.shape[1], text_feats.shape[1]
    embed = image_proj.shape[1]
    parts, pack = call(
        project_kernel,
        "project",
        (
            jax.ShapeDtypeStruct((groups, 2 * share, embed), BF16),
            jax.ShapeDtypeStruct((d_txt + d_img, HALF), BF16),
        ),
        (image_feats.T, text_feats, image_proj, text_proj),
        2 * rows * (d_img + d_txt) * embed,
    )
    lines = [pack] + [swapped(pack, "yl", bits) for bits in range(1, quad)]
    parts = lax.all_to_all(parts, X, 0, 0, tiled=True)
    summed = jnp.sum(parts.astype(F32), axis=0)
    length = jnp.sqrt(jnp.sum(summed * summed, axis=1, keepdims=True) + NORM_EPS)
    unit = summed / length
    emb = unit.astype(BF16)
    img_own, txt_own = emb[:share], emb[share:]
    img_all = jnp.broadcast_to(img_own[None], (groups, share, embed))
    img_all = lax.all_to_all(img_all, X, 0, 0, tiled=True).reshape(rows, embed)
    near = shifted(txt_own, 1)
    pair = jnp.concatenate([txt_own, near])
    far = shifted(pair, 2)
    cols = jnp.concatenate([pair, far])
    offsets = jnp.arange(STEPS, dtype=jnp.int32)
    col_ids = (
        jnp.mod(anchor - offsets, blocks)[:, None] * rows
        + member * share
        + jnp.arange(share, dtype=jnp.int32)[None, :]
    ).reshape(-1)
    scale_value, bias_value = logit_scale[0], logit_bias[0]
    polarity = jnp.where(labels[:, None] == col_ids[None, :], 1.0, -1.0).astype(F32)
    logits = (
        scale_value * lax.dot_general(img_all, cols, ACROSS, preferred_element_type=F32)
        + bias_value
    )
    weights = (-scale_value * polarity * jax.nn.sigmoid(-polarity * logits) / rows).astype(BF16)
    txt_terms = lax.dot_general(weights, img_all, DOWN, preferred_element_type=F32)
    img_terms = jnp.dot(weights, cols, preferred_element_type=F32).astype(BF16)
    back = shifted(txt_terms[2 * share :].astype(BF16), -2)
    img_terms = lax.all_to_all(img_terms.reshape(groups, share, embed), X, 0, 0, tiled=True)
    img_terms, lines = lax.optimization_barrier((img_terms, lines))
    two = txt_terms[: 2 * share] + back.astype(F32)
    last = shifted(two[share:].astype(BF16), -1)
    grad_txt = two[:share] + last.astype(F32)
    grad_img = jnp.sum(img_terms.astype(F32), axis=0)
    grad = jnp.concatenate([grad_img, grad_txt])
    grad_summed = ((grad - unit * jnp.sum(unit * grad, axis=1, keepdims=True)) / length).astype(BF16)
    strip = embed // (blocks // lax.axis_size("z"))
    by_cols = grad_summed.reshape(2, share, embed // (quad * strip), quad, strip)
    by_cols = by_cols.transpose(3, 1, 0, 2, 4).reshape(quad, share, 2 * embed // quad)
    by_cols = lax.all_to_all(by_cols, "yl", 0, 0, tiled=True)
    cols_all = lax.all_gather(by_cols, X, axis=0, tiled=False)
    height = 4 * embed // blocks
    wgrad = call(
        wgrad_kernel,
        "project_grads",
        jax.ShapeDtypeStruct((peers, height, HALF), BF16),
        (lax.axis_index("yl").astype(jnp.int32).reshape(1), cols_all, *lines),
        2 * quad * rows * (embed // quad) * (d_img + d_txt),
        scratch=(pltpu.VMEM((peers, height, HALF), F32),),
        scalars=1,
    )
    wgrad = lax.all_to_all(wgrad, ("yh", "z"), 0, 0, tiled=True)
    rows_all = lax.all_gather(grad_summed, X, axis=0, tiled=False)
    image_grad, text_grad = call(
        feature_grads_kernel,
        "feature_grads",
        (jax.ShapeDtypeStruct((d_img, rows), BF16), jax.ShapeDtypeStruct((rows, d_txt), BF16)),
        (rows_all, image_proj, text_proj),
        2 * rows * (d_img + d_txt) * embed,
    )
    img_wgrad, txt_wgrad = call(
        total_kernel,
        "total",
        (
            jax.ShapeDtypeStruct((embed // blocks, d_img), F32),
            jax.ShapeDtypeStruct((embed // blocks, d_txt), F32),
        ),
        (wgrad,),
        peers * height * HALF,
        scratch=(pltpu.VMEM((height, HALF), F32),),
    )
    return (image_grad.T, text_grad, img_wgrad.T, txt_wgrad.T)


def solution(mesh):
    fine = Mesh(mesh.devices.reshape(2, 4, 8, 2, 2, 2), DP + X)
    placed = (P(DP, X), P(DP, X), P(X, None), P(X, None), P(DP), P(), P())
    return jax.shard_map(
        on_device,
        mesh=fine,
        in_specs=placed,
        out_specs=(P(DP, X), P(DP, X), P(X, DP), P(X, DP)),
        check_vma=False,
    )
```

```python
import jax
import jax.numpy as jnp
from jax import lax
from jax.experimental import pallas as pl
from jax.experimental.pallas import tpu as pltpu
from jax.sharding import Mesh, PartitionSpec as P

STEPS = 4
NORM_EPS = 1e-06
CHIPS = ("xh", "xl")
X = CHIPS + ("core",)
Y = ("yh", "yl")
DP = ("yh", "yl", "z")
ACROSS = (((1,), (1,)), ((), ()))
DOWN = (((0,), (0,)), ((), ()))
HALF = 256
VMEM = 58 * 1024 * 1024
F32, BF16 = jnp.float32, jnp.bfloat16


def shifted(value, steps):
    count = lax.axis_size(DP)
    pairs = [(source, (source + steps) % count) for source in range(count)]
    return lax.ppermute(value, DP, pairs)


def along_y(value, steps):
    count = lax.axis_size(Y)
    pairs = [(source, (source + steps) % count) for source in range(count)]
    return lax.ppermute(value, Y, pairs)


def core_swapped(value):
    return lax.ppermute(value, "core", [(0, 1), (1, 0)])


def call(kernel, name, out_shape, args, flops, scratch=(), scalars=0):
    spaces = [pltpu.SMEM] * scalars + [pltpu.VMEM] * (len(args) - scalars)
    return pl.pallas_call(
        kernel,
        out_shape=out_shape,
        in_specs=[pl.BlockSpec(memory_space=space) for space in spaces],
        scratch_shapes=list(scratch),
        compiler_params=pltpu.CompilerParams(vmem_limit_bytes=VMEM),
        cost_estimate=pl.CostEstimate(flops=flops, bytes_accessed=4_000_000, transcendentals=0),
        name=name,
    )(*args)


def project_kernel(
    core_ref, img_t_ref, txt_ref, img_proj_ref, txt_proj_ref, mine_ref, other_ref, pack_ref, parts_ref
):
    groups, share = parts_ref.shape[0], parts_ref.shape[1] // 2
    d_txt = txt_ref.shape[1]
    for half in range(d_txt // HALF):
        pack_ref[half * HALF : (half + 1) * HALF] = txt_ref[:, half * HALF : (half + 1) * HALF]
    pack_ref[d_txt:] = img_t_ref[...]
    txt = jnp.dot(txt_ref[...], txt_proj_ref[...], preferred_element_type=F32).astype(BF16)
    img = lax.dot_general(img_t_ref[...], img_proj_ref[...], DOWN, preferred_element_type=F32)
    img = img.astype(BF16)
    for member in range(groups):
        rows = slice(member * share, (member + 1) * share)
        parts_ref[member, :share] = img[rows]
        parts_ref[member, share:] = txt[rows]
    core = core_ref[0]
    for chip in range(groups // 2):
        mine_ref[chip] = parts_ref[2 * chip + core]
        other_ref[chip] = parts_ref[2 * chip + 1 - core]


def wgrad_kernel(core_ref, mine_ref, other_ref, *refs):
    lines, out_ref, total_ref, cols_ref = refs[:-3], refs[-3], refs[-2], refs[-1]
    chips, height, wide = mine_ref.shape
    share = height // 8
    d_all = lines[0].shape[0]
    d_txt = 2 * HALF
    d_img = d_all - d_txt
    sums = [None] * 3
    for step, line_ref in enumerate(lines):
        for chip in range(chips):
            for ref, core in ((mine_ref, core_ref[0]), (other_ref, 1 - core_ref[0])):
                row = pl.multiple_of((2 * chip + core) * share, share)
                cols_ref[step, pl.ds(row, share)] = ref[chip, step * share : (step + 1) * share]
        cols = cols_ref[step].T
        img_cols, txt_cols = cols[: wide // 2], cols[wide // 2 :]
        terms = [
            jnp.dot(txt_cols, line_ref[:HALF], preferred_element_type=F32),
            jnp.dot(txt_cols, line_ref[HALF:d_txt], preferred_element_type=F32),
            lax.dot_general(img_cols, line_ref[d_txt:], ACROSS, preferred_element_type=F32),
        ]
        sums = [term if total is None else total + term for total, term in zip(sums, terms)]
    peers, height, _ = out_ref.shape
    take = height // 4
    for peer in range(peers):
        rows = slice(peer * take, (peer + 1) * take)
        total_ref[peer, :take] = sums[0][rows]
        total_ref[peer, take : 2 * take] = sums[1][rows]
        total_ref[peer, 2 * take : 3 * take] = sums[2][rows, :HALF]
        total_ref[peer, 3 * take :, : d_img - HALF] = sums[2][rows, HALF:]
        total_ref[peer, 3 * take :, d_img - HALF :] = jnp.zeros((take, 2 * HALF - d_img), F32)
    out_ref[...] = total_ref[...].astype(BF16)


def total_kernel(blocks_ref, img_ref, txt_ref, total_ref):
    take = img_ref.shape[0]
    d_img = img_ref.shape[1]
    total = blocks_ref[0].astype(F32)
    for peer in range(1, blocks_ref.shape[0]):
        total = total + blocks_ref[peer].astype(F32)
    total_ref[...] = total
    txt_ref[:, :HALF] = total_ref[:take]
    txt_ref[:, HALF:] = total_ref[take : 2 * take]
    img_ref[:, :HALF] = total_ref[2 * take : 3 * take]
    img_ref[:, HALF:] = total_ref[3 * take :, : d_img - HALF]


def feature_grads_kernel(
    core_ref, mine_ref, other_ref, img_proj_ref, txt_proj_ref, img_ref, txt_ref, img_rows, txt_rows
):
    chips, height, wide = mine_ref.shape
    share = height // 8
    for chip in range(chips):
        for ref, core in ((mine_ref, core_ref[0]), (other_ref, 1 - core_ref[0])):
            row = pl.multiple_of((2 * chip + core) * share, share)
            for part in range(2):
                lanes = slice(part * wide, (part + 1) * wide)
                first = (4 + 2 * part) * share
                img_rows[pl.ds(row, share), lanes] = ref[chip, first : first + share]
                txt_rows[pl.ds(row, share), lanes] = ref[chip, first + share : first + 2 * share]
    txt_ref[...] = lax.dot_general(
        txt_rows[...], txt_proj_ref[...], ACROSS, preferred_element_type=F32
    ).astype(BF16)
    img_ref[...] = lax.dot_general(
        img_proj_ref[...], img_rows[...], ACROSS, preferred_element_type=F32
    ).astype(BF16)


def on_device(image_feats, text_feats, image_proj, text_proj, labels, logit_scale, logit_bias):
    groups = lax.axis_size(X)
    member = lax.axis_index(X)
    anchor = lax.axis_index(DP)
    blocks = lax.axis_size(DP)
    quad = lax.axis_size("yl")
    peers = blocks // quad
    rows = image_feats.shape[0]
    share = rows // groups
    d_img, d_txt = image_feats.shape[1], text_feats.shape[1]
    embed = image_proj.shape[1]
    chips = lax.axis_size(CHIPS)
    core_index = lax.axis_index("core").astype(jnp.int32).reshape(1)
    halves = jax.ShapeDtypeStruct((chips, 2 * share, embed), BF16)
    mine, other, pack = call(
        project_kernel,
        "project",
        (halves, halves, jax.ShapeDtypeStruct((d_txt + d_img, HALF), BF16)),
        (core_index, image_feats.T, text_feats, image_proj, text_proj),
        2 * rows * (d_img + d_txt) * embed,
        scratch=(pltpu.VMEM((groups, 2 * share, embed), BF16),),
        scalars=1,
    )
    parts = (mine.astype(F32) + core_swapped(other).astype(F32)).astype(BF16)
    lines = [along_y(pack, 1), pack, along_y(pack, -1), along_y(pack, -2)]
    parts = lax.all_to_all(parts, CHIPS, 0, 0, tiled=True)
    summed = jnp.sum(parts.astype(F32), axis=0)
    length = jnp.sqrt(jnp.sum(summed * summed, axis=1, keepdims=True) + NORM_EPS)
    unit = summed / length
    emb = unit.astype(BF16)
    img_own, txt_own = emb[:share], emb[share:]
    img_all = jnp.broadcast_to(img_own[None], (groups, share, embed))
    img_all = lax.all_to_all(img_all, X, 0, 0, tiled=True).reshape(rows, embed)
    near = shifted(txt_own, 1)
    pair = jnp.concatenate([txt_own, near])
    far = shifted(pair, 2)
    cols = jnp.concatenate([pair, far])
    offsets = jnp.arange(STEPS, dtype=jnp.int32)
    col_ids = (
        jnp.mod(anchor - offsets, blocks)[:, None] * rows
        + member * share
        + jnp.arange(share, dtype=jnp.int32)[None, :]
    ).reshape(-1)
    scale_value, bias_value = logit_scale[0], logit_bias[0]
    polarity = jnp.where(labels[:, None] == col_ids[None, :], 1.0, -1.0).astype(F32)
    logits = (
        scale_value * lax.dot_general(img_all, cols, ACROSS, preferred_element_type=F32)
        + bias_value
    )
    weights = (-scale_value * polarity * jax.nn.sigmoid(-polarity * logits) / rows).astype(BF16)
    txt_terms = lax.dot_general(weights, img_all, DOWN, preferred_element_type=F32)
    img_terms = jnp.dot(weights, cols, preferred_element_type=F32).astype(BF16)
    back = shifted(txt_terms[2 * share :].astype(BF16), -2)
    img_terms = lax.all_to_all(img_terms.reshape(groups, share, embed), X, 0, 0, tiled=True)
    img_terms, lines = lax.optimization_barrier((img_terms, lines))
    two = txt_terms[: 2 * share] + back.astype(F32)
    last = shifted(two[share:].astype(BF16), -1)
    grad_txt = two[:share] + last.astype(F32)
    grad_img = jnp.sum(img_terms.astype(F32), axis=0)
    grad = jnp.concatenate([grad_img, grad_txt])
    grad_summed = ((grad - unit * jnp.sum(unit * grad, axis=1, keepdims=True)) / length).astype(BF16)
    strip = embed // lax.axis_size(Y)
    by_cols = grad_summed.reshape(2, share, embed // (quad * strip), quad, strip)
    by_cols = by_cols.transpose(3, 1, 0, 2, 4).reshape(quad, share, 2 * embed // quad)
    by_cols = jnp.concatenate([by_cols] * (lax.axis_size(Y) // quad))
    by_cols = lax.all_to_all(by_cols, Y, 0, 0, tiled=True)
    y_index = lax.axis_index(Y)
    window = [
        lax.dynamic_index_in_dim(by_cols, lax.rem(y_index + (step + lax.axis_size(Y)), lax.axis_size(Y)), 0, False)
        for step in (-1, 0, 1, 2)
    ]
    wide = 2 * embed // quad
    mine = jnp.concatenate(window + [grad_summed[:, :wide], grad_summed[:, wide:]])
    mine = jnp.broadcast_to(mine[None], (chips,) + mine.shape)
    mine = lax.all_to_all(mine, CHIPS, 0, 0, tiled=True)
    other = core_swapped(mine)
    height = 4 * embed // blocks
    wgrad = call(
        wgrad_kernel,
        "project_grads",
        jax.ShapeDtypeStruct((peers, height, HALF), BF16),
        (core_index, mine, other, *lines),
        2 * quad * rows * (embed // quad) * (d_img + d_txt),
        scratch=(pltpu.VMEM((peers, height, HALF), F32), pltpu.VMEM((quad, rows, wide), BF16)),
        scalars=1,
    )
    wgrad = lax.all_to_all(wgrad, ("yh", "z"), 0, 0, tiled=True)
    image_grad, text_grad = call(
        feature_grads_kernel,
        "feature_grads",
        (jax.ShapeDtypeStruct((d_img, rows), BF16), jax.ShapeDtypeStruct((rows, d_txt), BF16)),
        (core_index, mine, other, image_proj, text_proj),
        2 * rows * (d_img + d_txt) * embed,
        scratch=(pltpu.VMEM((rows, embed), BF16), pltpu.VMEM((rows, embed), BF16)),
        scalars=1,
    )
    img_wgrad, txt_wgrad = call(
        total_kernel,
        "total",
        (
            jax.ShapeDtypeStruct((embed // blocks, d_img), F32),
            jax.ShapeDtypeStruct((embed // blocks, d_txt), F32),
        ),
        (wgrad,),
        peers * height * HALF,
        scratch=(pltpu.VMEM((height, HALF), F32),),
    )
    return (image_grad.T, text_grad, img_wgrad.T, txt_wgrad.T)


def solution(mesh):
    fine = Mesh(mesh.devices.reshape(2, 4, 8, 2, 2, 2), DP + X)
    placed = (P(DP, X), P(DP, X), P(X, None), P(X, None), P(DP), P(), P())
    return jax.shard_map(
        on_device,
        mesh=fine,
        in_specs=placed,
        out_specs=(P(DP, X), P(DP, X), P(X, DP), P(X, DP)),
        check_vma=False,
    )
```

```python
import jax
import jax.numpy as jnp
from jax import lax
from jax.experimental import pallas as pl
from jax.experimental.pallas import tpu as pltpu
from jax.sharding import Mesh, PartitionSpec as P

STEPS = 4
NORM_EPS = 1e-06
CHIPS = ("xh", "xl")
X = CHIPS + ("core",)
Y = ("yh", "yl")
DP = ("yh", "yl", "z")
ACROSS = (((1,), (1,)), ((), ()))
DOWN = (((0,), (0,)), ((), ()))
HALF = 256
VMEM = 58 * 1024 * 1024
F32, BF16 = jnp.float32, jnp.bfloat16


def shifted(value, steps):
    count = lax.axis_size(DP)
    pairs = [(source, (source + steps) % count) for source in range(count)]
    return lax.ppermute(value, DP, pairs)


def along_y(value, steps):
    count = lax.axis_size(Y)
    pairs = [(source, (source + steps) % count) for source in range(count)]
    return lax.ppermute(value, Y, pairs)


def swapped(value, axis):
    return lax.ppermute(value, axis, [(0, 1), (1, 0)])


def core_swapped(value):
    return swapped(value, "core")


def call(kernel, name, out_shape, args, flops, scratch=(), scalars=0, vmem=VMEM):
    spaces = [pltpu.SMEM] * scalars + [pltpu.VMEM] * (len(args) - scalars)
    return pl.pallas_call(
        kernel,
        out_shape=out_shape,
        in_specs=[pl.BlockSpec(memory_space=space) for space in spaces],
        scratch_shapes=list(scratch),
        compiler_params=pltpu.CompilerParams(vmem_limit_bytes=vmem),
        cost_estimate=pl.CostEstimate(flops=flops, bytes_accessed=4_000_000, transcendentals=0),
        name=name,
    )(*args)


def project_kernel(img_t_ref, txt_ref, img_proj_ref, txt_proj_ref, parts_ref, pack_ref):
    groups, share = parts_ref.shape[0], parts_ref.shape[1] // 2
    d_txt = txt_ref.shape[1]
    for half in range(d_txt // HALF):
        pack_ref[half * HALF : (half + 1) * HALF] = txt_ref[:, half * HALF : (half + 1) * HALF]
    pack_ref[d_txt:] = img_t_ref[...]
    txt = jnp.dot(txt_ref[...], txt_proj_ref[...], preferred_element_type=F32).astype(BF16)
    img = lax.dot_general(img_t_ref[...], img_proj_ref[...], DOWN, preferred_element_type=F32)
    img = img.astype(BF16)
    for member in range(groups):
        rows = slice(member * share, (member + 1) * share)
        parts_ref[member, :share] = img[rows]
        parts_ref[member, share:] = txt[rows]


def wgrad_kernel(core_ref, mine_ref, other_ref, *refs):
    lines, out_ref, total_ref, cols_ref = refs[:-3], refs[-3], refs[-2], refs[-1]
    chips, height, wide = mine_ref.shape
    share = height // len(refs[:-3])
    d_all = lines[0].shape[0]
    d_txt = 2 * HALF
    d_img = d_all - d_txt
    sums = [None] * 3
    for step, line_ref in enumerate(lines):
        for chip in range(chips):
            for ref, core in ((mine_ref, core_ref[0]), (other_ref, 1 - core_ref[0])):
                row = pl.multiple_of((2 * chip + core) * share, share)
                cols_ref[step, pl.ds(row, share)] = ref[chip, step * share : (step + 1) * share]
        cols = cols_ref[step].T
        img_cols, txt_cols = cols[: wide // 2], cols[wide // 2 :]
        terms = [
            jnp.dot(txt_cols, line_ref[:HALF], preferred_element_type=F32),
            jnp.dot(txt_cols, line_ref[HALF:d_txt], preferred_element_type=F32),
            lax.dot_general(img_cols, line_ref[d_txt:], ACROSS, preferred_element_type=F32),
        ]
        sums = [term if total is None else total + term for total, term in zip(sums, terms)]
    peers, height, _ = out_ref.shape
    take = height // 4
    for peer in range(peers):
        rows = slice(peer * take, (peer + 1) * take)
        total_ref[peer, :take] = sums[0][rows]
        total_ref[peer, take : 2 * take] = sums[1][rows]
        total_ref[peer, 2 * take : 3 * take] = sums[2][rows, :HALF]
        total_ref[peer, 3 * take :, : d_img - HALF] = sums[2][rows, HALF:]
        total_ref[peer, 3 * take :, d_img - HALF :] = jnp.zeros((take, 2 * HALF - d_img), F32)
    out_ref[...] = total_ref[...].astype(BF16)


def total_kernel(blocks_ref, img_ref, txt_ref, total_ref):
    take = img_ref.shape[0]
    d_img = img_ref.shape[1]
    total = blocks_ref[0].astype(F32)
    for peer in range(1, blocks_ref.shape[0]):
        total = total + blocks_ref[peer].astype(F32)
    total_ref[...] = total
    txt_ref[:, :HALF] = total_ref[:take]
    txt_ref[:, HALF:] = total_ref[take : 2 * take]
    img_ref[:, :HALF] = total_ref[2 * take : 3 * take]
    img_ref[:, HALF:] = total_ref[3 * take :, : d_img - HALF]


def feature_grads_kernel(
    member_ref, own_ref, high_ref, low_ref, core_ref, img_proj_ref, txt_proj_ref,
    img_ref, txt_ref, img_rows, txt_rows,
):
    share = own_ref.shape[0] // 2
    places = iter((0, 4, 2, 6, 1, 5, 3, 7))
    for ref in (own_ref, high_ref, low_ref, core_ref):
        for piece in range(ref.shape[0] // (2 * share)):
            row = pl.multiple_of((member_ref[0] ^ next(places)) * share, share)
            first = piece * 2 * share
            img_rows[pl.ds(row, share)] = ref[first : first + share]
            txt_rows[pl.ds(row, share)] = ref[first + share : first + 2 * share]
    txt_ref[...] = lax.dot_general(
        txt_rows[...], txt_proj_ref[...], ACROSS, preferred_element_type=F32
    ).astype(txt_ref.dtype)
    img_ref[...] = lax.dot_general(
        img_proj_ref[...], img_rows[...], ACROSS, preferred_element_type=F32
    ).astype(img_ref.dtype)


def on_device(image_feats, text_feats, image_proj, text_proj, labels, logit_scale, logit_bias):
    groups = lax.axis_size(X)
    member = lax.axis_index(X)
    anchor = lax.axis_index(DP)
    blocks = lax.axis_size(DP)
    quad = lax.axis_size("yl")
    peers = blocks // quad
    rows = image_feats.shape[0]
    share = rows // groups
    d_img, d_txt = image_feats.shape[1], text_feats.shape[1]
    embed = image_proj.shape[1]
    chips = lax.axis_size(CHIPS)
    parts, pack = call(
        project_kernel,
        "project",
        (
            jax.ShapeDtypeStruct((groups, 2 * share, embed), BF16),
            jax.ShapeDtypeStruct((d_txt + d_img, HALF), BF16),
        ),
        (image_feats.T, text_feats, image_proj, text_proj),
        2 * rows * (d_img + d_txt) * embed,
    )
    below, above = along_y(pack, 1), along_y(pack, -1)
    parts = lax.all_to_all(parts, X, 0, 0, tiled=True)
    summed = jnp.sum(parts.astype(F32), axis=0)
    length = jnp.sqrt(jnp.sum(summed * summed, axis=1, keepdims=True) + NORM_EPS)
    unit = summed / length
    emb = unit.astype(BF16)
    img_own, txt_own = emb[:share], emb[share:]
    img_all = jnp.broadcast_to(img_own[None], (groups, share, embed))
    img_all = lax.all_to_all(img_all, X, 0, 0, tiled=True).reshape(rows, embed)
    near = shifted(txt_own, 1)
    pair = jnp.concatenate([txt_own, near])
    pair, below, above = lax.optimization_barrier((pair, below, above))
    far = shifted(pair, 2)
    lines = [below, pack, above, along_y(above, -1)]
    cols = jnp.concatenate([pair, far])
    offsets = jnp.arange(STEPS, dtype=jnp.int32)
    col_ids = (
        jnp.mod(anchor - offsets, blocks)[:, None] * rows
        + member * share
        + jnp.arange(share, dtype=jnp.int32)[None, :]
    ).reshape(-1)
    scale_value, bias_value = logit_scale[0], logit_bias[0]
    polarity = jnp.where(labels[:, None] == col_ids[None, :], 1.0, -1.0).astype(F32)
    logits = (
        scale_value * lax.dot_general(img_all, cols, ACROSS, preferred_element_type=F32)
        + bias_value
    )
    weights = (-scale_value * polarity * jax.nn.sigmoid(-polarity * logits) / rows).astype(BF16)
    txt_terms = lax.dot_general(weights, img_all, DOWN, preferred_element_type=F32)
    img_terms = jnp.dot(weights, cols, preferred_element_type=F32).astype(BF16)
    back = shifted(txt_terms[2 * share :].astype(BF16), -2)
    img_terms = lax.all_to_all(img_terms.reshape(groups, share, embed), X, 0, 0, tiled=True)
    img_terms, lines[3] = lax.optimization_barrier((img_terms, lines[3]))
    two = txt_terms[: 2 * share] + back.astype(F32)
    last = shifted(two[share:].astype(BF16), -1)
    grad_txt = two[:share] + last.astype(F32)
    grad_img = jnp.sum(img_terms.astype(F32), axis=0)
    grad = jnp.concatenate([grad_img, grad_txt])
    grad_summed = ((grad - unit * jnp.sum(unit * grad, axis=1, keepdims=True)) / length).astype(BF16)
    strip = embed // lax.axis_size(Y)
    by_cols = grad_summed.reshape(2, share, embed // (quad * strip), quad, strip)
    by_cols = by_cols.transpose(3, 1, 0, 2, 4).reshape(quad, share, 2 * embed // quad)
    by_cols = jnp.concatenate([by_cols] * (lax.axis_size(Y) // quad))
    by_cols = lax.all_to_all(by_cols, Y, 0, 0, tiled=True)
    pieces = [grad_summed, swapped(grad_summed, "xh")]
    by_cols, pieces = lax.optimization_barrier((by_cols, pieces))
    y_index = lax.axis_index(Y)
    window = [
        lax.dynamic_index_in_dim(by_cols, lax.rem(y_index + (step + lax.axis_size(Y)), lax.axis_size(Y)), 0, False)
        for step in (-1, 0, 1, 2)
    ]
    mine = jnp.concatenate(window)
    mine = jnp.broadcast_to(mine[None], (chips,) + mine.shape)
    mine = lax.all_to_all(mine, CHIPS, 0, 0, tiled=True)
    other = core_swapped(mine)
    pieces.append(swapped(jnp.concatenate(pieces), "xl"))
    pieces.append(core_swapped(jnp.concatenate(pieces)))
    wide = 2 * embed // quad
    height = 4 * embed // blocks
    wgrad = call(
        wgrad_kernel,
        "project_grads",
        jax.ShapeDtypeStruct((peers, height, HALF), BF16),
        (lax.axis_index("core").astype(jnp.int32).reshape(1), mine, other, *lines),
        2 * quad * rows * (embed // quad) * (d_img + d_txt),
        scratch=(pltpu.VMEM((peers, height, HALF), F32), pltpu.VMEM((quad, rows, wide), BF16)),
        scalars=1,
    )
    wgrad = lax.all_to_all(wgrad, ("yh", "z"), 0, 0, tiled=True)
    image_grad, text_grad = call(
        feature_grads_kernel,
        "feature_grads",
        (jax.ShapeDtypeStruct((d_img, rows), BF16), jax.ShapeDtypeStruct((rows, d_txt), BF16)),
        (member.astype(jnp.int32).reshape(1), *pieces, image_proj, text_proj),
        2 * rows * (d_img + d_txt) * embed,
        scratch=(pltpu.VMEM((rows, embed), BF16), pltpu.VMEM((rows, embed), BF16)),
        scalars=1,
    )
    img_wgrad, txt_wgrad = call(
        total_kernel,
        "total",
        (
            jax.ShapeDtypeStruct((embed // blocks, d_img), F32),
            jax.ShapeDtypeStruct((embed // blocks, d_txt), F32),
        ),
        (wgrad,),
        peers * height * HALF,
        scratch=(pltpu.VMEM((height, HALF), F32),),
        vmem=VMEM // 4,
    )
    return (image_grad.T, text_grad, img_wgrad.T, txt_wgrad.T)


def solution(mesh):
    fine = Mesh(mesh.devices.reshape(2, 4, 8, 2, 2, 2), DP + X)
    placed = (P(DP, X), P(DP, X), P(X, None), P(X, None), P(DP), P(), P())
    return jax.shard_map(
        on_device,
        mesh=fine,
        in_specs=placed,
        out_specs=(P(DP, X), P(DP, X), P(X, DP), P(X, DP)),
        check_vma=False,
    )
```

```python
import jax
import jax.numpy as jnp
from jax import lax
from jax.experimental import pallas as pl
from jax.experimental.pallas import tpu as pltpu
from jax.sharding import Mesh, PartitionSpec as P

STEPS = 4
NORM_EPS = 1e-06
CHIPS = ("xh", "xl")
X = CHIPS + ("core",)
Y = ("yq", "yp")
DP = Y + ("z",)
ACROSS = (((1,), (1,)), ((), ()))
DOWN = (((0,), (0,)), ((), ()))
HALF = 256
VMEM = 58 * 1024 * 1024
F32, BF16 = jnp.float32, jnp.bfloat16


def shifted(value, steps):
    count = lax.axis_size(DP)
    pairs = [(source, (source + steps) % count) for source in range(count)]
    return lax.ppermute(value, DP, pairs)


def along_y(value, steps):
    count = lax.axis_size(Y)
    sign = 1 if steps % 2 else -1
    pairs = [
        (source, (source + (sign * steps if source % 2 else -sign * steps)) % count)
        for source in range(count)
    ]
    return lax.ppermute(value, Y, pairs)


def swapped(value, axis):
    return lax.ppermute(value, axis, [(0, 1), (1, 0)])


def core_swapped(value):
    return swapped(value, "core")


def call(kernel, name, out_shape, args, flops, scratch=(), scalars=0, far=0, vmem=VMEM):
    near = len(args) - scalars - far
    spaces = [pltpu.SMEM] * scalars + [pltpu.VMEM] * near + [pltpu.HBM] * far
    return pl.pallas_call(
        kernel,
        out_shape=out_shape,
        in_specs=[pl.BlockSpec(memory_space=space) for space in spaces],
        scratch_shapes=list(scratch),
        compiler_params=pltpu.CompilerParams(vmem_limit_bytes=vmem),
        cost_estimate=pl.CostEstimate(flops=flops, bytes_accessed=4_000_000, transcendentals=0),
        name=name,
    )(*args)


def project_kernel(img_t_ref, txt_ref, img_proj_ref, txt_proj_ref, parts_ref, pack_ref):
    groups, share = parts_ref.shape[0], parts_ref.shape[1] // 2
    d_txt = txt_ref.shape[1]
    for half in range(d_txt // HALF):
        pack_ref[half * HALF : (half + 1) * HALF] = txt_ref[:, half * HALF : (half + 1) * HALF]
    pack_ref[d_txt:] = img_t_ref[...]
    txt = jnp.dot(txt_ref[...], txt_proj_ref[...], preferred_element_type=F32).astype(BF16)
    img = lax.dot_general(img_t_ref[...], img_proj_ref[...], DOWN, preferred_element_type=F32)
    img = img.astype(BF16)
    for member in range(groups):
        rows = slice(member * share, (member + 1) * share)
        parts_ref[member, :share] = img[rows]
        parts_ref[member, share:] = txt[rows]


def wgrad_kernel(core_ref, mine_ref, other_ref, *refs):
    far, (out_ref, total_ref, cols_ref, lines, sems) = refs[:-5], refs[-5:]
    copies = [
        pltpu.make_async_copy(ref, lines.at[step], sems.at[step]) for step, ref in enumerate(far)
    ]
    for copy in copies:
        copy.start()
    chips, height, wide = mine_ref.shape
    share = height // len(far)
    d_all = far[0].shape[0]
    d_txt = 2 * HALF
    d_img = d_all - d_txt
    sums = [None] * 3
    for step, copy in enumerate(copies):
        line_ref = lines.at[step]
        for chip in range(chips):
            for ref, core in ((mine_ref, core_ref[0]), (other_ref, 1 - core_ref[0])):
                row = pl.multiple_of((2 * chip + core) * share, share)
                cols_ref[step, pl.ds(row, share)] = ref[chip, step * share : (step + 1) * share]
        cols = cols_ref[step].T
        copy.wait()
        img_cols, txt_cols = cols[: wide // 2], cols[wide // 2 :]
        terms = [
            jnp.dot(txt_cols, line_ref[:HALF], preferred_element_type=F32),
            jnp.dot(txt_cols, line_ref[HALF:d_txt], preferred_element_type=F32),
            lax.dot_general(img_cols, line_ref[d_txt:], ACROSS, preferred_element_type=F32),
        ]
        sums = [term if total is None else total + term for total, term in zip(sums, terms)]
    peers, height, _ = out_ref.shape
    take = height // 4
    for peer in range(peers):
        rows = slice(peer * take, (peer + 1) * take)
        total_ref[peer, :take] = sums[0][rows]
        total_ref[peer, take : 2 * take] = sums[1][rows]
        total_ref[peer, 2 * take : 3 * take] = sums[2][rows, :HALF]
        total_ref[peer, 3 * take :, : d_img - HALF] = sums[2][rows, HALF:]
        total_ref[peer, 3 * take :, d_img - HALF :] = jnp.zeros((take, 2 * HALF - d_img), F32)
    out_ref[...] = total_ref[...].astype(BF16)


def total_kernel(blocks_ref, img_ref, txt_ref, total_ref):
    take = img_ref.shape[0]
    d_img = img_ref.shape[1]
    total = blocks_ref[0].astype(F32)
    for peer in range(1, blocks_ref.shape[0]):
        total = total + blocks_ref[peer].astype(F32)
    total_ref[...] = total
    txt_ref[:, :HALF] = total_ref[:take]
    txt_ref[:, HALF:] = total_ref[take : 2 * take]
    img_ref[:, :HALF] = total_ref[2 * take : 3 * take]
    img_ref[:, HALF:] = total_ref[3 * take :, : d_img - HALF]


def feature_grads_kernel(
    member_ref, own_ref, high_ref, low_ref, core_ref, img_proj_ref, txt_proj_ref,
    img_ref, txt_ref, img_rows, txt_rows,
):
    share = own_ref.shape[0] // 2
    places = iter((0, 4, 2, 6, 1, 5, 3, 7))
    for ref in (own_ref, high_ref, low_ref, core_ref):
        for piece in range(ref.shape[0] // (2 * share)):
            row = pl.multiple_of((member_ref[0] ^ next(places)) * share, share)
            first = piece * 2 * share
            img_rows[pl.ds(row, share)] = ref[first : first + share]
            txt_rows[pl.ds(row, share)] = ref[first + share : first + 2 * share]
    txt_ref[...] = lax.dot_general(
        txt_rows[...], txt_proj_ref[...], ACROSS, preferred_element_type=F32
    ).astype(txt_ref.dtype)
    img_ref[...] = lax.dot_general(
        img_proj_ref[...], img_rows[...], ACROSS, preferred_element_type=F32
    ).astype(img_ref.dtype)


def on_device(image_feats, text_feats, image_proj, text_proj, labels, logit_scale, logit_bias):
    groups = lax.axis_size(X)
    member = lax.axis_index(X)
    anchor = lax.axis_index(DP)
    blocks = lax.axis_size(DP)
    quad = lax.axis_size("yq")
    peers = blocks // quad
    rows = image_feats.shape[0]
    share = rows // groups
    d_img, d_txt = image_feats.shape[1], text_feats.shape[1]
    embed = image_proj.shape[1]
    chips = lax.axis_size(CHIPS)
    parts, pack = call(
        project_kernel,
        "project",
        (
            jax.ShapeDtypeStruct((groups, 2 * share, embed), BF16),
            jax.ShapeDtypeStruct((d_txt + d_img, HALF), BF16),
        ),
        (image_feats.T, text_feats, image_proj, text_proj),
        2 * rows * (d_img + d_txt) * embed,
    )
    second = along_y(pack, 1)
    parts = lax.all_to_all(parts, X, 0, 0, tiled=True)
    summed = jnp.sum(parts.astype(F32), axis=0)
    length = jnp.sqrt(jnp.sum(summed * summed, axis=1, keepdims=True) + NORM_EPS)
    unit = summed / length
    emb = unit.astype(BF16)
    img_own, txt_own = emb[:share], emb[share:]
    img_all = jnp.broadcast_to(img_own[None], (groups, share, embed))
    img_all = lax.all_to_all(img_all, X, 0, 0, tiled=True).reshape(rows, embed)
    near = shifted(txt_own, 1)
    pair = jnp.concatenate([txt_own, near])
    pair, second, held = lax.optimization_barrier((pair, second, pack))
    far = shifted(pair, 2)
    third = along_y(held, 2)
    cols = jnp.concatenate([pair, far])
    offsets = jnp.arange(STEPS, dtype=jnp.int32)
    col_ids = (
        jnp.mod(anchor - offsets, blocks)[:, None] * rows
        + member * share
        + jnp.arange(share, dtype=jnp.int32)[None, :]
    ).reshape(-1)
    scale_value, bias_value = logit_scale[0], logit_bias[0]
    polarity = jnp.where(labels[:, None] == col_ids[None, :], 1.0, -1.0).astype(F32)
    logits = (
        scale_value * lax.dot_general(img_all, cols, ACROSS, preferred_element_type=F32)
        + bias_value
    )
    weights = (-scale_value * polarity * jax.nn.sigmoid(-polarity * logits) / rows).astype(BF16)
    txt_terms = lax.dot_general(weights, img_all, DOWN, preferred_element_type=F32)
    img_terms = jnp.dot(weights, cols, preferred_element_type=F32).astype(BF16)
    back = shifted(txt_terms[2 * share :].astype(BF16), -2)
    img_terms = lax.all_to_all(img_terms.reshape(groups, share, embed), X, 0, 0, tiled=True)
    img_terms, third = lax.optimization_barrier((img_terms, third))
    two = txt_terms[: 2 * share] + back.astype(F32)
    last = shifted(two[share:].astype(BF16), -1)
    grad_txt = two[:share] + last.astype(F32)
    grad_img = jnp.sum(img_terms.astype(F32), axis=0)
    grad = jnp.concatenate([grad_img, grad_txt])
    grad_summed = ((grad - unit * jnp.sum(unit * grad, axis=1, keepdims=True)) / length).astype(BF16)
    wide = embed // quad
    by_cols = grad_summed.reshape(2, share, quad, 1, wide).transpose(2, 3, 1, 0, 4)
    by_cols = jnp.broadcast_to(by_cols, (quad, lax.axis_size("yp"), share, 2, wide))
    by_cols = by_cols.reshape(lax.axis_size(Y), share, 2 * wide)
    by_cols = lax.all_to_all(by_cols, Y, 0, 0, tiled=True)
    pieces = [grad_summed, swapped(grad_summed, "xh")]
    by_cols, pieces = lax.optimization_barrier((by_cols, pieces))
    y_index = lax.axis_index(Y)
    sign = 2 * lax.axis_index("yp") - 1
    window = [
        lax.dynamic_index_in_dim(by_cols, (y_index + sign * step) & (lax.axis_size(Y) - 1), 0, False)
        for step in range(quad)
    ]
    mine = jnp.concatenate(window)
    mine, second = lax.optimization_barrier((mine, second))
    lines = [pack, second, third, along_y(second, 2)]
    mine = jnp.broadcast_to(mine[None], (chips,) + mine.shape)
    mine = lax.all_to_all(mine, CHIPS, 0, 0, tiled=True)
    other = core_swapped(mine)
    pieces.append(swapped(jnp.concatenate(pieces), "xl"))
    pieces.append(core_swapped(jnp.concatenate(pieces)))
    height = 4 * embed // blocks
    wgrad = call(
        wgrad_kernel,
        "project_grads",
        jax.ShapeDtypeStruct((peers, height, HALF), BF16),
        (lax.axis_index("core").astype(jnp.int32).reshape(1), mine, other, *lines),
        2 * quad * rows * (embed // quad) * (d_img + d_txt),
        scratch=(
            pltpu.VMEM((peers, height, HALF), F32),
            pltpu.VMEM((quad, rows, 2 * wide), BF16),
            pltpu.VMEM((quad, d_txt + d_img, HALF), BF16),
            pltpu.SemaphoreType.DMA((quad,)),
        ),
        scalars=1,
        far=quad,
        vmem=VMEM // 4,
    )
    wgrad = lax.all_to_all(wgrad, ("yp", "z"), 0, 0, tiled=True)
    image_grad, text_grad = call(
        feature_grads_kernel,
        "feature_grads",
        (jax.ShapeDtypeStruct((d_img, rows), BF16), jax.ShapeDtypeStruct((rows, d_txt), BF16)),
        (member.astype(jnp.int32).reshape(1), *pieces, image_proj, text_proj),
        2 * rows * (d_img + d_txt) * embed,
        scratch=(pltpu.VMEM((rows, embed), BF16), pltpu.VMEM((rows, embed), BF16)),
        scalars=1,
        vmem=VMEM // 4,
    )
    img_wgrad, txt_wgrad = call(
        total_kernel,
        "total",
        (
            jax.ShapeDtypeStruct((embed // blocks, d_img), F32),
            jax.ShapeDtypeStruct((embed // blocks, d_txt), F32),
        ),
        (wgrad,),
        peers * height * HALF,
        scratch=(pltpu.VMEM((height, HALF), F32),),
        vmem=VMEM // 4,
    )
    return (image_grad.T, text_grad, img_wgrad.T, txt_wgrad.T)


def solution(mesh):
    fine = Mesh(mesh.devices.reshape(4, 2, 8, 2, 2, 2), DP + X)
    placed = (P(DP, X), P(DP, X), P(X, None), P(X, None), P(DP), P(), P())
    return jax.shard_map(
        on_device,
        mesh=fine,
        in_specs=placed,
        out_specs=(P(DP, X), P(DP, X), P(X, DP), P(X, DP)),
        check_vma=False,
    )
```

```python
import jax
import jax.numpy as jnp
from jax import lax
from jax.experimental import pallas as pl
from jax.experimental.pallas import tpu as pltpu
from jax.sharding import Mesh, PartitionSpec as P

STEPS = 4
NORM_EPS = 1e-06
CHIPS = ("xh", "xl")
X = CHIPS + ("core",)
Y = ("yq", "yp")
DP = Y + ("z",)
ACROSS = (((1,), (1,)), ((), ()))
DOWN = (((0,), (0,)), ((), ()))
HALF = 256
VMEM = 58 * 1024 * 1024
F32, BF16 = jnp.float32, jnp.bfloat16


def shifted(value, steps):
    count = lax.axis_size(DP)
    pairs = [(source, (source + steps) % count) for source in range(count)]
    return lax.ppermute(value, DP, pairs)


def along_y(value, steps):
    count = lax.axis_size(Y)
    sign = 1 if steps % 2 else -1
    pairs = [
        (source, (source + (sign * steps if source % 2 else -sign * steps)) % count)
        for source in range(count)
    ]
    return lax.ppermute(value, Y, pairs)


def swapped(value, axis):
    return lax.ppermute(value, axis, [(0, 1), (1, 0)])


def core_swapped(value):
    return swapped(value, "core")


def call(kernel, name, out_shape, args, flops, scratch=(), scalars=0, far=0, vmem=VMEM):
    near = len(args) - scalars - far
    spaces = [pltpu.SMEM] * scalars + [pltpu.VMEM] * near + [pltpu.HBM] * far
    return pl.pallas_call(
        kernel,
        out_shape=out_shape,
        in_specs=[pl.BlockSpec(memory_space=space) for space in spaces],
        scratch_shapes=list(scratch),
        compiler_params=pltpu.CompilerParams(vmem_limit_bytes=vmem),
        cost_estimate=pl.CostEstimate(flops=flops, bytes_accessed=4_000_000, transcendentals=0),
        name=name,
    )(*args)


def project_kernel(img_t_ref, txt_ref, img_proj_ref, txt_proj_ref, parts_ref, pack_ref):
    groups, share = parts_ref.shape[0], parts_ref.shape[1] // 2
    d_txt = txt_ref.shape[1]
    for half in range(d_txt // HALF):
        pack_ref[half * HALF : (half + 1) * HALF] = txt_ref[:, half * HALF : (half + 1) * HALF]
    pack_ref[d_txt:] = img_t_ref[...]
    txt = jnp.dot(txt_ref[...], txt_proj_ref[...], preferred_element_type=F32).astype(BF16)
    img = lax.dot_general(img_t_ref[...], img_proj_ref[...], DOWN, preferred_element_type=F32)
    img = img.astype(BF16)
    for member in range(groups):
        rows = slice(member * share, (member + 1) * share)
        parts_ref[member, :share] = img[rows]
        parts_ref[member, share:] = txt[rows]


def row_grads_kernel(summed_ref, img_ref, txt_ref, last_ref, rows_ref, cols_ref):
    share = last_ref.shape[0]
    wide = cols_ref.shape[2] // 2
    grad_img = img_ref[0].astype(F32)
    for member in range(1, img_ref.shape[0]):
        grad_img = grad_img + img_ref[member].astype(F32)
    grad_txt = txt_ref[:share] + last_ref[...].astype(F32)
    for tower, grad in enumerate((grad_img, grad_txt)):
        rows = slice(tower * share, (tower + 1) * share)
        summed = summed_ref[rows]
        length = jnp.sqrt(jnp.sum(summed * summed, axis=1, keepdims=True) + NORM_EPS)
        unit = summed / length
        grad = (grad - unit * jnp.sum(unit * grad, axis=1, keepdims=True)) / length
        grad = grad.astype(BF16)
        rows_ref[rows] = grad
        for block in range(cols_ref.shape[0]):
            quarter = slice(block // 2 * wide, (block // 2 + 1) * wide)
            cols_ref[block, :, tower * wide : (tower + 1) * wide] = grad[:, quarter]


def wgrad_kernel(core_ref, mine_ref, other_ref, *refs):
    far, (out_ref, total_ref, cols_ref, lines, sems) = refs[:-5], refs[-5:]
    copies = [
        pltpu.make_async_copy(ref, lines.at[step], sems.at[step]) for step, ref in enumerate(far)
    ]
    for copy in copies:
        copy.start()
    chips, height, wide = mine_ref.shape
    share = height // len(far)
    d_all = far[0].shape[0]
    d_txt = 2 * HALF
    d_img = d_all - d_txt
    sums = [None] * 3
    for step, copy in enumerate(copies):
        line_ref = lines.at[step]
        for chip in range(chips):
            for ref, core in ((mine_ref, core_ref[0]), (other_ref, 1 - core_ref[0])):
                row = pl.multiple_of((2 * chip + core) * share, share)
                cols_ref[step, pl.ds(row, share)] = ref[chip, step * share : (step + 1) * share]
        cols = cols_ref[step].T
        copy.wait()
        img_cols, txt_cols = cols[: wide // 2], cols[wide // 2 :]
        terms = [
            jnp.dot(txt_cols, line_ref[:HALF], preferred_element_type=F32),
            jnp.dot(txt_cols, line_ref[HALF:d_txt], preferred_element_type=F32),
            lax.dot_general(img_cols, line_ref[d_txt:], ACROSS, preferred_element_type=F32),
        ]
        sums = [term if total is None else total + term for total, term in zip(sums, terms)]
    peers, height, _ = out_ref.shape
    take = height // 4
    for peer in range(peers):
        rows = slice(peer * take, (peer + 1) * take)
        total_ref[peer, :take] = sums[0][rows]
        total_ref[peer, take : 2 * take] = sums[1][rows]
        total_ref[peer, 2 * take : 3 * take] = sums[2][rows, :HALF]
        total_ref[peer, 3 * take :, : d_img - HALF] = sums[2][rows, HALF:]
        total_ref[peer, 3 * take :, d_img - HALF :] = jnp.zeros((take, 2 * HALF - d_img), F32)
    out_ref[...] = total_ref[...].astype(BF16)


def total_kernel(blocks_ref, img_ref, txt_ref, total_ref):
    take = img_ref.shape[0]
    d_img = img_ref.shape[1]
    total = blocks_ref[0].astype(F32)
    for peer in range(1, blocks_ref.shape[0]):
        total = total + blocks_ref[peer].astype(F32)
    total_ref[...] = total
    txt_ref[:, :HALF] = total_ref[:take]
    txt_ref[:, HALF:] = total_ref[take : 2 * take]
    img_ref[:, :HALF] = total_ref[2 * take : 3 * take]
    img_ref[:, HALF:] = total_ref[3 * take :, : d_img - HALF]


def feature_grads_kernel(
    member_ref, own_ref, high_ref, low_ref, core_ref, img_proj_ref, txt_proj_ref,
    img_ref, txt_ref, img_rows, txt_rows,
):
    share = own_ref.shape[0] // 2
    places = iter((0, 4, 2, 6, 1, 5, 3, 7))
    for ref in (own_ref, high_ref, low_ref, core_ref):
        for piece in range(ref.shape[0] // (2 * share)):
            row = pl.multiple_of((member_ref[0] ^ next(places)) * share, share)
            first = piece * 2 * share
            img_rows[pl.ds(row, share)] = ref[first : first + share]
            txt_rows[pl.ds(row, share)] = ref[first + share : first + 2 * share]
    txt_ref[...] = lax.dot_general(
        txt_rows[...], txt_proj_ref[...], ACROSS, preferred_element_type=F32
    ).astype(txt_ref.dtype)
    img_ref[...] = lax.dot_general(
        img_proj_ref[...], img_rows[...], ACROSS, preferred_element_type=F32
    ).astype(img_ref.dtype)


def on_device(image_feats, text_feats, image_proj, text_proj, labels, logit_scale, logit_bias):
    groups = lax.axis_size(X)
    member = lax.axis_index(X)
    anchor = lax.axis_index(DP)
    blocks = lax.axis_size(DP)
    quad = lax.axis_size("yq")
    peers = blocks // quad
    rows = image_feats.shape[0]
    share = rows // groups
    d_img, d_txt = image_feats.shape[1], text_feats.shape[1]
    embed = image_proj.shape[1]
    chips = lax.axis_size(CHIPS)
    parts, pack = call(
        project_kernel,
        "project",
        (
            jax.ShapeDtypeStruct((groups, 2 * share, embed), BF16),
            jax.ShapeDtypeStruct((d_txt + d_img, HALF), BF16),
        ),
        (image_feats.T, text_feats, image_proj, text_proj),
        2 * rows * (d_img + d_txt) * embed,
    )
    second = along_y(pack, 1)
    parts = lax.all_to_all(parts, X, 0, 0, tiled=True)
    offsets = jnp.arange(STEPS, dtype=jnp.int32)
    col_ids = (
        jnp.mod(anchor - offsets, blocks)[:, None] * rows
        + member * share
        + jnp.arange(share, dtype=jnp.int32)[None, :]
    ).reshape(-1)
    scale_value, bias_value = logit_scale[0], logit_bias[0]
    parts, col_ids, scale_value, bias_value = lax.optimization_barrier(
        (parts, col_ids, scale_value, bias_value)
    )
    summed = jnp.sum(parts.astype(F32), axis=0)
    length = jnp.sqrt(jnp.sum(summed * summed, axis=1, keepdims=True) + NORM_EPS)
    unit = summed / length
    emb = unit.astype(BF16)
    img_own, txt_own = emb[:share], emb[share:]
    img_all = jnp.broadcast_to(img_own[None], (groups, share, embed))
    img_all = lax.all_to_all(img_all, X, 0, 0, tiled=True).reshape(rows, embed)
    near = shifted(txt_own, 1)
    pair = jnp.concatenate([txt_own, near])
    pair, second, held = lax.optimization_barrier((pair, second, pack))
    far = shifted(pair, 2)
    third = along_y(held, 2)
    cols = jnp.concatenate([pair, far])
    polarity = jnp.where(labels[:, None] == col_ids[None, :], 1.0, -1.0).astype(F32)
    logits = (
        scale_value * lax.dot_general(img_all, cols, ACROSS, preferred_element_type=F32)
        + bias_value
    )
    weights = (-scale_value * polarity * jax.nn.sigmoid(-polarity * logits) / rows).astype(BF16)
    txt_terms = lax.dot_general(weights, img_all, DOWN, preferred_element_type=F32)
    img_terms = jnp.dot(weights, cols, preferred_element_type=F32).astype(BF16)
    back = shifted(txt_terms[2 * share :].astype(BF16), -2)
    img_terms = lax.all_to_all(img_terms.reshape(groups, share, embed), X, 0, 0, tiled=True)
    img_terms, third = lax.optimization_barrier((img_terms, third))
    two = txt_terms[: 2 * share] + back.astype(F32)
    last = shifted(two[share:].astype(BF16), -1)
    wide = embed // quad
    grad_summed, by_cols = call(
        row_grads_kernel,
        "row_grads",
        (
            jax.ShapeDtypeStruct((2 * share, embed), BF16),
            jax.ShapeDtypeStruct((lax.axis_size(Y), share, 2 * wide), BF16),
        ),
        (summed, img_terms, two, last),
        groups * share * embed,
        vmem=VMEM // 4,
    )
    by_cols = lax.all_to_all(by_cols, Y, 0, 0, tiled=True)
    pieces = [grad_summed, swapped(grad_summed, "xh")]
    by_cols, pieces = lax.optimization_barrier((by_cols, pieces))
    y_index = lax.axis_index(Y)
    sign = 2 * lax.axis_index("yp") - 1
    window = [
        lax.dynamic_index_in_dim(by_cols, (y_index + sign * step) & (lax.axis_size(Y) - 1), 0, False)
        for step in range(quad)
    ]
    mine = jnp.concatenate(window)
    mine, second = lax.optimization_barrier((mine, second))
    lines = [pack, second, third, along_y(second, 2)]
    mine = jnp.broadcast_to(mine[None], (chips,) + mine.shape)
    mine = lax.all_to_all(mine, CHIPS, 0, 0, tiled=True)
    other = core_swapped(mine)
    pieces.append(swapped(jnp.concatenate(pieces), "xl"))
    pieces.append(core_swapped(jnp.concatenate(pieces)))
    height = 4 * embed // blocks
    wgrad = call(
        wgrad_kernel,
        "project_grads",
        jax.ShapeDtypeStruct((peers, height, HALF), BF16),
        (lax.axis_index("core").astype(jnp.int32).reshape(1), mine, other, *lines),
        2 * quad * rows * (embed // quad) * (d_img + d_txt),
        scratch=(
            pltpu.VMEM((peers, height, HALF), F32),
            pltpu.VMEM((quad, rows, 2 * wide), BF16),
            pltpu.VMEM((quad, d_txt + d_img, HALF), BF16),
            pltpu.SemaphoreType.DMA((quad,)),
        ),
        scalars=1,
        far=quad,
        vmem=VMEM // 4,
    )
    wgrad = lax.all_to_all(wgrad, ("yp", "z"), 0, 0, tiled=True)
    image_grad, text_grad = call(
        feature_grads_kernel,
        "feature_grads",
        (jax.ShapeDtypeStruct((d_img, rows), BF16), jax.ShapeDtypeStruct((rows, d_txt), BF16)),
        (member.astype(jnp.int32).reshape(1), *pieces, image_proj, text_proj),
        2 * rows * (d_img + d_txt) * embed,
        scratch=(pltpu.VMEM((rows, embed), BF16), pltpu.VMEM((rows, embed), BF16)),
        scalars=1,
        vmem=VMEM // 4,
    )
    img_wgrad, txt_wgrad = call(
        total_kernel,
        "total",
        (
            jax.ShapeDtypeStruct((embed // blocks, d_img), F32),
            jax.ShapeDtypeStruct((embed // blocks, d_txt), F32),
        ),
        (wgrad,),
        peers * height * HALF,
        scratch=(pltpu.VMEM((height, HALF), F32),),
        vmem=VMEM // 4,
    )
    return (image_grad.T, text_grad, img_wgrad.T, txt_wgrad.T)


def solution(mesh):
    fine = Mesh(mesh.devices.reshape(4, 2, 8, 2, 2, 2), DP + X)
    placed = (P(DP, X), P(DP, X), P(X, None), P(X, None), P(DP), P(), P())
    return jax.shard_map(
        on_device,
        mesh=fine,
        in_specs=placed,
        out_specs=(P(DP, X), P(DP, X), P(X, DP), P(X, DP)),
        check_vma=False,
    )
```

```python
import jax
import jax.numpy as jnp
from jax import lax
from jax.experimental import pallas as pl
from jax.experimental.pallas import tpu as pltpu
from jax.sharding import Mesh, PartitionSpec as P

STEPS = 4
NORM_EPS = 1e-06
CHIPS = ("xh", "xl")
X = CHIPS + ("core",)
Y = ("yq", "yp")
DP = Y + ("z",)
ACROSS = (((1,), (1,)), ((), ()))
DOWN = (((0,), (0,)), ((), ()))
HALF = 256
VMEM = 58 * 1024 * 1024
F32, BF16 = jnp.float32, jnp.bfloat16


def shifted(value, steps):
    count = lax.axis_size(DP)
    pairs = [(source, (source + steps) % count) for source in range(count)]
    return lax.ppermute(value, DP, pairs)


def along_y(value, steps):
    count = lax.axis_size(Y)
    sign = 1 if steps % 2 else -1
    pairs = [
        (source, (source + (sign * steps if source % 2 else -sign * steps)) % count)
        for source in range(count)
    ]
    return lax.ppermute(value, Y, pairs)


def swapped(value, axis):
    return lax.ppermute(value, axis, [(0, 1), (1, 0)])


def core_swapped(value):
    return swapped(value, "core")


def call(kernel, name, out_shape, args, flops, scratch=(), scalars=0, far=0, vmem=VMEM):
    near = len(args) - scalars - far
    spaces = [pltpu.SMEM] * scalars + [pltpu.VMEM] * near + [pltpu.HBM] * far
    return pl.pallas_call(
        kernel,
        out_shape=out_shape,
        in_specs=[pl.BlockSpec(memory_space=space) for space in spaces],
        scratch_shapes=list(scratch),
        compiler_params=pltpu.CompilerParams(vmem_limit_bytes=vmem),
        cost_estimate=pl.CostEstimate(flops=flops, bytes_accessed=4_000_000, transcendentals=0),
        name=name,
    )(*args)


def project_kernel(img_t_ref, txt_ref, img_proj_ref, txt_proj_ref, parts_ref, pack_ref):
    groups, share = parts_ref.shape[0], parts_ref.shape[1] // 2
    d_txt = txt_ref.shape[1]
    for half in range(d_txt // HALF):
        pack_ref[half * HALF : (half + 1) * HALF] = txt_ref[:, half * HALF : (half + 1) * HALF]
    pack_ref[d_txt:] = img_t_ref[...]
    txt = jnp.dot(txt_ref[...], txt_proj_ref[...], preferred_element_type=F32).astype(BF16)
    img = lax.dot_general(img_t_ref[...], img_proj_ref[...], DOWN, preferred_element_type=F32)
    img = img.astype(BF16)
    for member in range(groups):
        rows = slice(member * share, (member + 1) * share)
        parts_ref[member, :share] = img[rows]
        parts_ref[member, share:] = txt[rows]


def row_grads_kernel(summed_ref, img_ref, txt_ref, last_ref, rows_ref, cols_ref):
    share = last_ref.shape[0]
    wide = cols_ref.shape[2] // 2
    grad_img = img_ref[0].astype(F32)
    for member in range(1, img_ref.shape[0]):
        grad_img = grad_img + img_ref[member].astype(F32)
    grad_txt = txt_ref[:share] + last_ref[...].astype(F32)
    for tower, grad in enumerate((grad_img, grad_txt)):
        rows = slice(tower * share, (tower + 1) * share)
        summed = summed_ref[rows]
        length = jnp.sqrt(jnp.sum(summed * summed, axis=1, keepdims=True) + NORM_EPS)
        unit = summed / length
        grad = (grad - unit * jnp.sum(unit * grad, axis=1, keepdims=True)) / length
        grad = grad.astype(BF16)
        rows_ref[rows] = grad
        for block in range(cols_ref.shape[0]):
            quarter = slice(block // 2 * wide, (block // 2 + 1) * wide)
            cols_ref[block, :, tower * wide : (tower + 1) * wide] = grad[:, quarter]


def wgrad_kernel(core_ref, mine_ref, other_ref, *refs):
    far, (out_ref, total_ref, cols_ref, lines, sems) = refs[:-5], refs[-5:]
    copies = [
        pltpu.make_async_copy(ref, lines.at[step], sems.at[step]) for step, ref in enumerate(far)
    ]
    for copy in copies:
        copy.start()
    chips, height, wide = mine_ref.shape
    share = height // len(far)
    d_all = far[0].shape[0]
    d_txt = 2 * HALF
    d_img = d_all - d_txt
    for step in range(len(copies)):
        for chip in range(chips):
            for ref, core in ((mine_ref, core_ref[0]), (other_ref, 1 - core_ref[0])):
                row = pl.multiple_of((2 * chip + core) * share, share)
                cols_ref[step, pl.ds(row, share)] = ref[chip, step * share : (step + 1) * share]
    cols = jnp.concatenate([cols_ref[step].T for step in range(len(copies))], axis=1)
    img_cols, txt_cols = cols[: wide // 2], cols[wide // 2 :]
    for copy in copies:
        copy.wait()
    sums = [
        jnp.dot(
            txt_cols,
            lines[:, half * HALF : (half + 1) * HALF].reshape(cols.shape[1], HALF),
            preferred_element_type=F32,
        )
        for half in range(2)
    ]
    img_lines = jnp.concatenate([lines[step, d_txt:] for step in range(len(copies))], axis=1)
    sums.append(lax.dot_general(img_cols, img_lines, ACROSS, preferred_element_type=F32))
    peers, height, _ = out_ref.shape
    take = height // 4
    for peer in range(peers):
        rows = slice(peer * take, (peer + 1) * take)
        total_ref[peer, :take] = sums[0][rows]
        total_ref[peer, take : 2 * take] = sums[1][rows]
        total_ref[peer, 2 * take : 3 * take] = sums[2][rows, :HALF]
        total_ref[peer, 3 * take :, : d_img - HALF] = sums[2][rows, HALF:]
        total_ref[peer, 3 * take :, d_img - HALF :] = jnp.zeros((take, 2 * HALF - d_img), F32)
    out_ref[...] = total_ref[...].astype(BF16)


def total_kernel(blocks_ref, img_ref, txt_ref, total_ref):
    take = img_ref.shape[0]
    d_img = img_ref.shape[1]
    total = blocks_ref[0].astype(F32)
    for peer in range(1, blocks_ref.shape[0]):
        total = total + blocks_ref[peer].astype(F32)
    total_ref[...] = total
    txt_ref[:, :HALF] = total_ref[:take]
    txt_ref[:, HALF:] = total_ref[take : 2 * take]
    img_ref[:, :HALF] = total_ref[2 * take : 3 * take]
    img_ref[:, HALF:] = total_ref[3 * take :, : d_img - HALF]


def feature_grads_kernel(
    member_ref, own_ref, high_ref, low_ref, core_ref, img_proj_ref, txt_proj_ref,
    img_ref, txt_ref, img_rows, txt_rows,
):
    share = own_ref.shape[0] // 2
    places = iter((0, 4, 2, 6, 1, 5, 3, 7))
    for ref in (own_ref, high_ref, low_ref, core_ref):
        for piece in range(ref.shape[0] // (2 * share)):
            row = pl.multiple_of((member_ref[0] ^ next(places)) * share, share)
            first = piece * 2 * share
            img_rows[pl.ds(row, share)] = ref[first : first + share]
            txt_rows[pl.ds(row, share)] = ref[first + share : first + 2 * share]
    txt_ref[...] = lax.dot_general(
        txt_rows[...], txt_proj_ref[...], ACROSS, preferred_element_type=F32
    ).astype(txt_ref.dtype)
    img_ref[...] = lax.dot_general(
        img_proj_ref[...], img_rows[...], ACROSS, preferred_element_type=F32
    ).astype(img_ref.dtype)


def on_device(image_feats, text_feats, image_proj, text_proj, labels, logit_scale, logit_bias):
    groups = lax.axis_size(X)
    member = lax.axis_index(X)
    anchor = lax.axis_index(DP)
    blocks = lax.axis_size(DP)
    quad = lax.axis_size("yq")
    peers = blocks // quad
    rows = image_feats.shape[0]
    share = rows // groups
    d_img, d_txt = image_feats.shape[1], text_feats.shape[1]
    embed = image_proj.shape[1]
    chips = lax.axis_size(CHIPS)
    parts, pack = call(
        project_kernel,
        "project",
        (
            jax.ShapeDtypeStruct((groups, 2 * share, embed), BF16),
            jax.ShapeDtypeStruct((d_txt + d_img, HALF), BF16),
        ),
        (image_feats.T, text_feats, image_proj, text_proj),
        2 * rows * (d_img + d_txt) * embed,
    )
    second = along_y(pack, 1)
    parts = lax.all_to_all(parts, X, 0, 0, tiled=True)
    offsets = jnp.array([0, 2, 1, 3], jnp.int32)
    col_ids = (
        jnp.mod(anchor - offsets, blocks)[:, None] * rows
        + member * share
        + jnp.arange(share, dtype=jnp.int32)[None, :]
    ).reshape(-1)
    scale_value, bias_value = logit_scale[0], logit_bias[0]
    parts, col_ids, scale_value, bias_value = lax.optimization_barrier(
        (parts, col_ids, scale_value, bias_value)
    )
    summed = jnp.sum(parts.astype(F32), axis=0)
    length = jnp.sqrt(jnp.sum(summed * summed, axis=1, keepdims=True) + NORM_EPS)
    unit = summed / length
    emb = unit.astype(BF16)
    img_own, txt_own = emb[:share], emb[share:]
    img_all = jnp.broadcast_to(img_own[None], (groups, share, embed))
    img_all = lax.all_to_all(img_all, X, 0, 0, tiled=True).reshape(rows, embed)
    near = shifted(txt_own, 1)
    pair = jnp.concatenate([txt_own, near])
    pair, second, held = lax.optimization_barrier((pair, second, pack))
    far = shifted(pair, 2)
    third = along_y(held, 2)
    cols = jnp.concatenate([txt_own, far[:share], near, far[share:]])
    polarity = jnp.where(labels[:, None] == col_ids[None, :], 1.0, -1.0).astype(F32)
    logits = (
        scale_value * lax.dot_general(img_all, cols, ACROSS, preferred_element_type=F32)
        + bias_value
    )
    weights = (-scale_value * polarity * jax.nn.sigmoid(-polarity * logits) / rows).astype(BF16)
    txt_terms = lax.dot_general(weights, img_all, DOWN, preferred_element_type=F32)
    img_terms = jnp.dot(weights, cols, preferred_element_type=F32).astype(BF16)
    back = shifted(txt_terms[2 * share :].astype(BF16), -1)
    img_terms = lax.all_to_all(img_terms.reshape(groups, share, embed), X, 0, 0, tiled=True)
    img_terms, third = lax.optimization_barrier((img_terms, third))
    two = txt_terms[: 2 * share] + back.astype(F32)
    last = shifted(two[share:].astype(BF16), -2)
    wide = embed // quad
    grad_summed, by_cols = call(
        row_grads_kernel,
        "row_grads",
        (
            jax.ShapeDtypeStruct((2 * share, embed), BF16),
            jax.ShapeDtypeStruct((lax.axis_size(Y), share, 2 * wide), BF16),
        ),
        (summed, img_terms, two, last),
        groups * share * embed,
        vmem=VMEM // 4,
    )
    by_cols = lax.all_to_all(by_cols, Y, 0, 0, tiled=True)
    pieces = [grad_summed, swapped(grad_summed, "xh")]
    by_cols, pieces = lax.optimization_barrier((by_cols, pieces))
    y_index = lax.axis_index(Y)
    sign = 2 * lax.axis_index("yp") - 1
    window = [
        lax.dynamic_index_in_dim(by_cols, (y_index + sign * step) & (lax.axis_size(Y) - 1), 0, False)
        for step in range(quad)
    ]
    mine = jnp.concatenate(window)
    mine, second = lax.optimization_barrier((mine, second))
    lines = [pack, second, third, along_y(second, 2)]
    mine = jnp.broadcast_to(mine[None], (chips,) + mine.shape)
    mine = lax.all_to_all(mine, CHIPS, 0, 0, tiled=True)
    other = core_swapped(mine)
    pieces.append(swapped(jnp.concatenate(pieces), "xl"))
    pieces.append(core_swapped(jnp.concatenate(pieces)))
    height = 4 * embed // blocks
    wgrad = call(
        wgrad_kernel,
        "project_grads",
        jax.ShapeDtypeStruct((peers, height, HALF), BF16),
        (lax.axis_index("core").astype(jnp.int32).reshape(1), mine, other, *lines),
        2 * quad * rows * (embed // quad) * (d_img + d_txt),
        scratch=(
            pltpu.VMEM((peers, height, HALF), F32),
            pltpu.VMEM((quad, rows, 2 * wide), BF16),
            pltpu.VMEM((quad, d_txt + d_img, HALF), BF16),
            pltpu.SemaphoreType.DMA((quad,)),
        ),
        scalars=1,
        far=quad,
        vmem=VMEM // 4,
    )
    wgrad = lax.all_to_all(wgrad, ("yp", "z"), 0, 0, tiled=True)
    image_grad, text_grad = call(
        feature_grads_kernel,
        "feature_grads",
        (jax.ShapeDtypeStruct((d_img, rows), BF16), jax.ShapeDtypeStruct((rows, d_txt), BF16)),
        (member.astype(jnp.int32).reshape(1), *pieces, image_proj, text_proj),
        2 * rows * (d_img + d_txt) * embed,
        scratch=(pltpu.VMEM((rows, embed), BF16), pltpu.VMEM((rows, embed), BF16)),
        scalars=1,
        vmem=VMEM // 4,
    )
    img_wgrad, txt_wgrad = call(
        total_kernel,
        "total",
        (
            jax.ShapeDtypeStruct((embed // blocks, d_img), F32),
            jax.ShapeDtypeStruct((embed // blocks, d_txt), F32),
        ),
        (wgrad,),
        peers * height * HALF,
        scratch=(pltpu.VMEM((height, HALF), F32),),
        vmem=VMEM // 4,
    )
    return (image_grad.T, text_grad, img_wgrad.T, txt_wgrad.T)


def solution(mesh):
    fine = Mesh(mesh.devices.reshape(4, 2, 8, 2, 2, 2), DP + X)
    placed = (P(DP, X), P(DP, X), P(X, None), P(X, None), P(DP), P(), P())
    return jax.shard_map(
        on_device,
        mesh=fine,
        in_specs=placed,
        out_specs=(P(DP, X), P(DP, X), P(X, DP), P(X, DP)),
        check_vma=False,
    )
```

```python
import jax
import jax.numpy as jnp
from jax import lax
from jax.experimental import pallas as pl
from jax.experimental.pallas import tpu as pltpu
from jax.sharding import Mesh, PartitionSpec as P

STEPS = 4
NORM_EPS = 1e-06
CHIPS = ("xh", "xl")
X = CHIPS + ("core",)
Y = ("yq", "yp")
DP = Y + ("z",)
ACROSS = (((1,), (1,)), ((), ()))
DOWN = (((0,), (0,)), ((), ()))
HALF = 256
VMEM = 58 * 1024 * 1024
F32, BF16 = jnp.float32, jnp.bfloat16


def shifted(value, steps):
    count = lax.axis_size(DP)
    pairs = [(source, (source + steps) % count) for source in range(count)]
    return lax.ppermute(value, DP, pairs)


def along_y(value, steps):
    count = lax.axis_size(Y)
    sign = 1 if steps % 2 else -1
    pairs = [
        (source, (source + (sign * steps if source % 2 else -sign * steps)) % count)
        for source in range(count)
    ]
    return lax.ppermute(value, Y, pairs)


def swapped(value, axis):
    return lax.ppermute(value, axis, [(0, 1), (1, 0)])


def core_swapped(value):
    return swapped(value, "core")


def call(kernel, name, out_shape, args, flops, scratch=(), scalars=0, far=0, vmem=VMEM):
    near = len(args) - scalars - far
    spaces = [pltpu.SMEM] * scalars + [pltpu.VMEM] * near + [pltpu.HBM] * far
    return pl.pallas_call(
        kernel,
        out_shape=out_shape,
        in_specs=[pl.BlockSpec(memory_space=space) for space in spaces],
        scratch_shapes=list(scratch),
        compiler_params=pltpu.CompilerParams(vmem_limit_bytes=vmem),
        cost_estimate=pl.CostEstimate(flops=flops, bytes_accessed=4_000_000, transcendentals=0),
        name=name,
    )(*args)


def project_kernel(scale_ref, bias_ref, img_t_ref, txt_ref, img_proj_ref, txt_proj_ref, parts_ref, pack_ref, scalars_ref):
    groups, share = parts_ref.shape[0], parts_ref.shape[1] // 2
    scalars_ref[:1] = jnp.full((1, scalars_ref.shape[1]), scale_ref[0], F32)
    scalars_ref[1:] = jnp.full((1, scalars_ref.shape[1]), bias_ref[0], F32)
    d_txt = txt_ref.shape[1]
    for half in range(d_txt // HALF):
        pack_ref[half * HALF : (half + 1) * HALF] = txt_ref[:, half * HALF : (half + 1) * HALF]
    pack_ref[d_txt:] = img_t_ref[...]
    txt = jnp.dot(txt_ref[...], txt_proj_ref[...], preferred_element_type=F32).astype(BF16)
    img = lax.dot_general(img_t_ref[...], img_proj_ref[...], DOWN, preferred_element_type=F32)
    img = img.astype(BF16)
    for member in range(groups):
        rows = slice(member * share, (member + 1) * share)
        parts_ref[member, :share] = img[rows]
        parts_ref[member, share:] = txt[rows]


def row_grads_kernel(summed_ref, img_ref, txt_ref, last_ref, rows_ref, cols_ref):
    share = last_ref.shape[0]
    wide = cols_ref.shape[2] // 2
    grad_img = img_ref[0].astype(F32)
    for member in range(1, img_ref.shape[0]):
        grad_img = grad_img + img_ref[member].astype(F32)
    grad_txt = txt_ref[:share] + last_ref[...].astype(F32)
    for tower, grad in enumerate((grad_img, grad_txt)):
        rows = slice(tower * share, (tower + 1) * share)
        summed = summed_ref[rows]
        length = jnp.sqrt(jnp.sum(summed * summed, axis=1, keepdims=True) + NORM_EPS)
        unit = summed / length
        grad = (grad - unit * jnp.sum(unit * grad, axis=1, keepdims=True)) / length
        grad = grad.astype(BF16)
        rows_ref[rows] = grad
        for block in range(cols_ref.shape[0]):
            quarter = slice(block // 2 * wide, (block // 2 + 1) * wide)
            cols_ref[block, :, tower * wide : (tower + 1) * wide] = grad[:, quarter]


def wgrad_kernel(core_ref, mine_ref, other_ref, *refs):
    far, (out_ref, total_ref, cols_ref, lines, sems) = refs[:-5], refs[-5:]
    copies = [
        pltpu.make_async_copy(ref, lines.at[step], sems.at[step]) for step, ref in enumerate(far)
    ]
    for copy in copies:
        copy.start()
    chips, height, wide = mine_ref.shape
    share = height // len(far)
    d_all = far[0].shape[0]
    d_txt = 2 * HALF
    d_img = d_all - d_txt
    for step in range(len(copies)):
        for chip in range(chips):
            for ref, core in ((mine_ref, core_ref[0]), (other_ref, 1 - core_ref[0])):
                row = pl.multiple_of((2 * chip + core) * share, share)
                cols_ref[step, pl.ds(row, share)] = ref[chip, step * share : (step + 1) * share]
    cols = jnp.concatenate([cols_ref[step].T for step in range(len(copies))], axis=1)
    img_cols, txt_cols = cols[: wide // 2], cols[wide // 2 :]
    for copy in copies:
        copy.wait()
    sums = [
        jnp.dot(
            txt_cols,
            lines[:, half * HALF : (half + 1) * HALF].reshape(cols.shape[1], HALF),
            preferred_element_type=F32,
        )
        for half in range(2)
    ]
    img_lines = jnp.concatenate([lines[step, d_txt:] for step in range(len(copies))], axis=1)
    sums.append(lax.dot_general(img_cols, img_lines, ACROSS, preferred_element_type=F32))
    peers, height, _ = out_ref.shape
    take = height // 4
    for peer in range(peers):
        rows = slice(peer * take, (peer + 1) * take)
        total_ref[peer, :take] = sums[0][rows]
        total_ref[peer, take : 2 * take] = sums[1][rows]
        total_ref[peer, 2 * take : 3 * take] = sums[2][rows, :HALF]
        total_ref[peer, 3 * take :, : d_img - HALF] = sums[2][rows, HALF:]
        total_ref[peer, 3 * take :, d_img - HALF :] = jnp.zeros((take, 2 * HALF - d_img), F32)
    out_ref[...] = total_ref[...].astype(BF16)


def total_kernel(blocks_ref, img_ref, txt_ref, total_ref):
    take = img_ref.shape[0]
    d_img = img_ref.shape[1]
    total = blocks_ref[0].astype(F32)
    for peer in range(1, blocks_ref.shape[0]):
        total = total + blocks_ref[peer].astype(F32)
    total_ref[...] = total
    txt_ref[:, :HALF] = total_ref[:take]
    txt_ref[:, HALF:] = total_ref[take : 2 * take]
    img_ref[:, :HALF] = total_ref[2 * take : 3 * take]
    img_ref[:, HALF:] = total_ref[3 * take :, : d_img - HALF]


def feature_grads_kernel(
    member_ref, own_ref, high_ref, low_ref, core_ref, img_proj_ref, txt_proj_ref,
    img_ref, txt_ref, img_rows, txt_rows,
):
    share = own_ref.shape[0] // 2
    places = iter((0, 4, 2, 6, 1, 5, 3, 7))
    for ref in (own_ref, high_ref, low_ref, core_ref):
        for piece in range(ref.shape[0] // (2 * share)):
            row = pl.multiple_of((member_ref[0] ^ next(places)) * share, share)
            first = piece * 2 * share
            img_rows[pl.ds(row, share)] = ref[first : first + share]
            txt_rows[pl.ds(row, share)] = ref[first + share : first + 2 * share]
    txt_ref[...] = lax.dot_general(
        txt_rows[...], txt_proj_ref[...], ACROSS, preferred_element_type=F32
    ).astype(txt_ref.dtype)
    img_ref[...] = lax.dot_general(
        img_proj_ref[...], img_rows[...], ACROSS, preferred_element_type=F32
    ).astype(img_ref.dtype)


def on_device(image_feats, text_feats, image_proj, text_proj, labels, logit_scale, logit_bias):
    groups = lax.axis_size(X)
    member = lax.axis_index(X)
    anchor = lax.axis_index(DP)
    blocks = lax.axis_size(DP)
    quad = lax.axis_size("yq")
    peers = blocks // quad
    rows = image_feats.shape[0]
    share = rows // groups
    d_img, d_txt = image_feats.shape[1], text_feats.shape[1]
    embed = image_proj.shape[1]
    chips = lax.axis_size(CHIPS)
    parts, pack, scalars = call(
        project_kernel,
        "project",
        (
            jax.ShapeDtypeStruct((groups, 2 * share, embed), BF16),
            jax.ShapeDtypeStruct((d_txt + d_img, HALF), BF16),
            jax.ShapeDtypeStruct((2, STEPS * share), F32),
        ),
        (logit_scale, logit_bias, image_feats.T, text_feats, image_proj, text_proj),
        2 * rows * (d_img + d_txt) * embed,
        scalars=2,
    )
    second = along_y(pack, 1)
    parts = lax.all_to_all(parts, X, 0, 0, tiled=True)
    offsets = jnp.array([0, 2, 1, 3], jnp.int32)
    col_ids = (
        jnp.mod(anchor - offsets, blocks)[:, None] * rows
        + member * share
        + jnp.arange(share, dtype=jnp.int32)[None, :]
    ).reshape(-1)
    scale_value, bias_value = scalars[:1], scalars[1:]
    parts, col_ids = lax.optimization_barrier((parts, col_ids))
    summed = jnp.sum(parts.astype(F32), axis=0)
    length = jnp.sqrt(jnp.sum(summed * summed, axis=1, keepdims=True) + NORM_EPS)
    unit = summed / length
    emb = unit.astype(BF16)
    img_own, txt_own = emb[:share], emb[share:]
    img_all = jnp.broadcast_to(img_own[None], (groups, share, embed))
    img_all = lax.all_to_all(img_all, X, 0, 0, tiled=True).reshape(rows, embed)
    near = shifted(txt_own, 1)
    pair = jnp.concatenate([txt_own, near])
    pair, second, held, col_ids = lax.optimization_barrier((pair, second, pack, col_ids))
    far = shifted(pair, 2)
    polarity = jnp.where(labels[:, None] == col_ids[None, :], 1.0, -1.0).astype(F32)
    held, polarity = lax.optimization_barrier((held, polarity))
    third = along_y(held, 2)
    cols = jnp.concatenate([txt_own, far[:share], near, far[share:]])
    logits = (
        scale_value * lax.dot_general(img_all, cols, ACROSS, preferred_element_type=F32)
        + bias_value
    )
    weights = (-scale_value * polarity * jax.nn.sigmoid(-polarity * logits) / rows).astype(BF16)
    txt_terms = lax.dot_general(weights, img_all, DOWN, preferred_element_type=F32)
    img_terms = jnp.dot(weights, cols, preferred_element_type=F32).astype(BF16)
    back = shifted(txt_terms[2 * share :].astype(BF16), -1)
    img_terms = lax.all_to_all(img_terms.reshape(groups, share, embed), X, 0, 0, tiled=True)
    img_terms, third = lax.optimization_barrier((img_terms, third))
    two = txt_terms[: 2 * share] + back.astype(F32)
    last = shifted(two[share:].astype(BF16), -2)
    wide = embed // quad
    grad_summed, by_cols = call(
        row_grads_kernel,
        "row_grads",
        (
            jax.ShapeDtypeStruct((2 * share, embed), BF16),
            jax.ShapeDtypeStruct((lax.axis_size(Y), share, 2 * wide), BF16),
        ),
        (summed, img_terms, two, last),
        groups * share * embed,
        vmem=VMEM // 4,
    )
    by_cols = lax.all_to_all(by_cols, Y, 0, 0, tiled=True)
    pieces = [grad_summed, swapped(grad_summed, "xh")]
    by_cols, pieces = lax.optimization_barrier((by_cols, pieces))
    y_index = lax.axis_index(Y)
    sign = 2 * lax.axis_index("yp") - 1
    window = [
        lax.dynamic_index_in_dim(by_cols, (y_index + sign * step) & (lax.axis_size(Y) - 1), 0, False)
        for step in range(quad)
    ]
    mine = jnp.concatenate(window)
    mine, second = lax.optimization_barrier((mine, second))
    lines = [pack, second, third, along_y(second, 2)]
    mine = jnp.broadcast_to(mine[None], (chips,) + mine.shape)
    mine = lax.all_to_all(mine, CHIPS, 0, 0, tiled=True)
    other = core_swapped(mine)
    pieces.append(swapped(jnp.concatenate(pieces), "xl"))
    pieces.append(core_swapped(jnp.concatenate(pieces)))
    height = 4 * embed // blocks
    wgrad = call(
        wgrad_kernel,
        "project_grads",
        jax.ShapeDtypeStruct((peers, height, HALF), BF16),
        (lax.axis_index("core").astype(jnp.int32).reshape(1), mine, other, *lines),
        2 * quad * rows * (embed // quad) * (d_img + d_txt),
        scratch=(
            pltpu.VMEM((peers, height, HALF), F32),
            pltpu.VMEM((quad, rows, 2 * wide), BF16),
            pltpu.VMEM((quad, d_txt + d_img, HALF), BF16),
            pltpu.SemaphoreType.DMA((quad,)),
        ),
        scalars=1,
        far=quad,
        vmem=VMEM // 4,
    )
    wgrad = lax.all_to_all(wgrad, ("yp", "z"), 0, 0, tiled=True)
    image_grad, text_grad = call(
        feature_grads_kernel,
        "feature_grads",
        (jax.ShapeDtypeStruct((d_img, rows), BF16), jax.ShapeDtypeStruct((rows, d_txt), BF16)),
        (member.astype(jnp.int32).reshape(1), *pieces, image_proj, text_proj),
        2 * rows * (d_img + d_txt) * embed,
        scratch=(pltpu.VMEM((rows, embed), BF16), pltpu.VMEM((rows, embed), BF16)),
        scalars=1,
        vmem=VMEM // 4,
    )
    img_wgrad, txt_wgrad = call(
        total_kernel,
        "total",
        (
            jax.ShapeDtypeStruct((embed // blocks, d_img), F32),
            jax.ShapeDtypeStruct((embed // blocks, d_txt), F32),
        ),
        (wgrad,),
        peers * height * HALF,
        scratch=(pltpu.VMEM((height, HALF), F32),),
        vmem=VMEM // 4,
    )
    return (image_grad.T, text_grad, img_wgrad.T, txt_wgrad.T)


def solution(mesh):
    fine = Mesh(mesh.devices.reshape(4, 2, 8, 2, 2, 2), DP + X)
    placed = (P(DP, X), P(DP, X), P(X, None), P(X, None), P(DP), P(), P())
    return jax.shard_map(
        on_device,
        mesh=fine,
        in_specs=placed,
        out_specs=(P(DP, X), P(DP, X), P(X, DP), P(X, DP)),
        check_vma=False,
    )
```
